256 devices in a mesh: enc: 32 (over z_lo, x, core), tp: 8 (over z_hi, y).
Axes of the slice: x: 4, y: 4, z: 8 (z_hi: 2, z_lo: 4; z = z_hi * 4 + z_lo), core: 2. Of those that a mesh axis runs over, the one named last changes fastest.
Arguments:
- vit_hidden: bfloat16 [2, 14336, 4608], P(None, ('enc', 'tp')), may hold values from -6 to 6
- merge_weight: bfloat16 [2, 4608, 5120], P(None, 'enc', 'tp'), may hold values from -0.09375 to 0.09375
- merge_bias: bfloat16 [2, 5120], P(None, 'tp'), may hold values from -3 to 3
- residual: bfloat16 [2, 65536, 5120], P(None, ('enc', 'tp')), may hold values from -6 to 6
- norm_gain: bfloat16 [2, 5120], replicated, may hold values from 0.5 to 1.5
- image_sequence: int32 [896], P('enc'), may hold values from 0 to 31, as said below
- token_source: int32 [65536], P('enc'), may hold values from -1 to 1023, as said below
Outputs:
- normed: bfloat16 [2, 65536, 5120], P(None, ('enc', 'tp'))
The draws below stay inside these ranges and needn't reach their ends.
Inputs may be any that keep to these rules, and one draw needn't show every extreme that they name: `image_sequence`: each encoder shard assigns at most 2 images to one sequence, and exactly 2 to some sequence in every draw; every sequence receives exactly 28 images. `token_source`: consistent with image_sequence: every image's 16 rows appear once, at 16 consecutive tokens of its own sequence, in row order; images do not intersect; all other tokens are -1.
All inputs are finite; a program needn't handle non-finite values.
Results may differ from the reference program's by a relative error of at most 0.0036.
Values may be sent and summed in bfloat16 or wider, within the bound.
A program may use at most 128 MiB of HBM per device.

```python
import jax
import jax.numpy as jnp
from jax import lax

LM_WIDTH = 5120
MERGE_IN = 4608
LEVELS = 2
IMG = 16
IMGS_DEV = 28
CAP = 2
SEQ = 2048
ROWS = 14336
TOKENS = 65536
N_ENC = 32


def image_layout(key):
    key_offsets, key_perm, key_order, key_cuts = jax.random.split(key, 4)
    doubled = IMGS_DEV // 2 - 1
    distinct = IMGS_DEV - doubled
    values_all = jnp.arange(N_ENC, dtype=jnp.int32)
    priority = jax.random.randint(key_offsets, (N_ENC,), 0, 1 << 20) * N_ENC + values_all
    priority = jnp.where(values_all == N_ENC // 2, -3, priority)
    priority = jnp.where(values_all == 1, -2, priority)
    priority = jnp.where(values_all == N_ENC - 1, -1, priority)
    chosen = jnp.argsort(priority, stable=True).astype(jnp.int32)[:distinct]
    offsets = jnp.concatenate([chosen, chosen[:doubled]]).astype(jnp.int32)
    slots = jnp.arange(IMGS_DEV, dtype=jnp.int32)
    scores = jax.random.randint(key_perm, (N_ENC, IMGS_DEV), 0, 1 << 20) * IMGS_DEV + slots[None, :]
    perm = jnp.argsort(scores, axis=1, stable=True).astype(jnp.int32)
    shard = jnp.broadcast_to(jnp.arange(N_ENC, dtype=jnp.int32)[:, None], (N_ENC, IMGS_DEV))
    target = ((shard + offsets[None, :]) % N_ENC).astype(jnp.int32)
    sequence_of = jnp.zeros((N_ENC, IMGS_DEV), jnp.int32).at[shard, perm].set(target)
    same = sequence_of[:, :, None] == sequence_of[:, None, :]
    earlier = slots[None, :] < slots[:, None]
    rank = jnp.sum(jnp.logical_and(same, earlier[None, :, :]), axis=2).astype(jnp.int32)
    order_scores = jax.random.randint(key_order, (N_ENC, IMGS_DEV), 0, 1 << 20) * IMGS_DEV + slots[None, :]
    placement = jnp.argsort(order_scores, axis=1, stable=True).astype(jnp.int32)
    text = SEQ - IMGS_DEV * IMG
    cuts = jnp.sort(jax.random.randint(key_cuts, (N_ENC, IMGS_DEV), 0, text + 1), axis=1).astype(jnp.int32)
    position = placement[target, slots[None, :]]
    start = cuts[target, position] + position * IMG
    image_rank = rank[shard, perm]
    within = jnp.arange(IMG, dtype=jnp.int32)
    tokens_at = (target * SEQ + start)[:, :, None] + within[None, None, :]
    values = (shard * CAP * IMG + image_rank * IMG)[:, :, None] + within[None, None, :]
    source = jnp.full((N_ENC * SEQ,), -1, jnp.int32).at[tokens_at.reshape(-1)].set(values.reshape(-1))
    return (sequence_of.reshape(-1), source)


def draw_image_sequence(key, part):
    sequence_of, source = image_layout(key)
    return sequence_of


def draw_token_source(key, part):
    sequence_of, source = image_layout(key)
    return source


def levels(key, shape, cuts, least, largest):
    def one(dim, parts):
        steps = jax.random.uniform(jax.random.fold_in(jax.random.fold_in(key, 6), dim), (parts,), jnp.float32, least / len(cuts), largest / len(cuts))
        return jnp.repeat(jnp.exp(steps), shape[dim] // parts).reshape((-1,) + (1,) * (len(shape) - dim - 1))

    gain = one(*cuts[0])
    for cut in cuts[1:]:
        gain = gain * one(*cut)
    return gain


def gaussian(own_key, extent, spread, limit, shards=(), held_as=jnp.bfloat16):
    level = levels(own_key, extent, shards, -0.22, 0.18) if shards else 1.0
    entries = jax.random.normal(own_key, extent, jnp.float32) * spread * level
    return jnp.minimum(jnp.maximum(entries, -limit), limit).astype(held_as)


def setup_inputs(seed: int = 0) -> dict:
    arg_keys = jax.random.split(jax.random.key(seed), 8)
    vit_hidden = gaussian(arg_keys[0], (LEVELS, ROWS, MERGE_IN), 1.0, 6.0, ((1, 256),))
    merge_weight = gaussian(arg_keys[1], (LEVELS, MERGE_IN, LM_WIDTH), MERGE_IN ** -0.5, 0.09375, ((1, 32), (2, 8)))
    merge_bias = gaussian(arg_keys[2], (LEVELS, LM_WIDTH), 0.5, 3.0, ((1, 8),))
    residual = gaussian(arg_keys[3], (LEVELS, TOKENS, LM_WIDTH), 1.0, 6.0, ((1, 256),))
    norm_gain = jnp.clip(1.0 + 0.1 * jax.random.normal(arg_keys[4], (LEVELS, LM_WIDTH), jnp.float32), 0.5, 1.5).astype(jnp.bfloat16)
    image_sequence = draw_image_sequence(jax.random.fold_in(arg_keys[7], 71), 0)
    token_source = draw_token_source(jax.random.fold_in(arg_keys[7], 71), 0)
    return {"vit_hidden": vit_hidden, "merge_weight": merge_weight, "merge_bias": merge_bias, "residual": residual, "norm_gain": norm_gain, "image_sequence": image_sequence, "token_source": token_source}


def image_table(image_sequence):
    grid = image_sequence.reshape(N_ENC, IMGS_DEV).astype(jnp.int32)
    same = grid[:, :, None] == grid[:, None, :]
    order = jnp.arange(IMGS_DEV, dtype=jnp.int32)
    earlier = order[None, :] < order[:, None]
    rank = lax.optimization_barrier(jnp.sum(jnp.logical_and(same, earlier[None, :, :]), axis=2)).astype(jnp.int32)
    shard = jnp.broadcast_to(jnp.arange(N_ENC, dtype=jnp.int32)[:, None], (N_ENC, IMGS_DEV))
    index = (shard * IMGS_DEV + order[None, :]).astype(jnp.int32)
    table = jnp.zeros((N_ENC, N_ENC, CAP), jnp.int32)
    return table.at[shard, grid, rank].set(index)

def reference(vit_hidden, merge_weight, merge_bias, residual, norm_gain, image_sequence, token_source):
    table = image_table(image_sequence)
    valid = token_source >= 0
    source = jnp.where(valid, token_source, 0).astype(jnp.int32)
    shard = (source // (CAP * IMG)).astype(jnp.int32)
    rank = (source // IMG % CAP).astype(jnp.int32)
    within = (source % IMG).astype(jnp.int32)
    sequence = (jnp.arange(TOKENS, dtype=jnp.int32) // SEQ).astype(jnp.int32)
    image = table[shard, sequence, rank]
    row = (image * IMG + within).astype(jnp.int32)
    results = []
    for level in range(LEVELS):
        projected = jnp.dot(vit_hidden[level], merge_weight[level], preferred_element_type=jnp.float32)
        merged = (projected + merge_bias[level].astype(jnp.float32)).astype(jnp.bfloat16)
        deep = jnp.where(valid[:, None], jnp.take(merged, row, axis=0), jnp.zeros((), jnp.bfloat16))
        updated = (residual[level].astype(jnp.float32) + deep.astype(jnp.float32)).astype(jnp.bfloat16)
        values = lax.optimization_barrier(updated).astype(jnp.float32)
        scale = lax.rsqrt(lax.optimization_barrier(jnp.mean(values * values, axis=-1, keepdims=True)) + 1e-06)
        results.append((values * scale * norm_gain[level].astype(jnp.float32)).astype(jnp.bfloat16))
    return jnp.stack(results)
```

```python
import functools

import jax
import jax.numpy as jnp
from jax import lax
from jax.experimental import pallas as pl
from jax.experimental.pallas import tpu as pltpu
from jax.sharding import PartitionSpec as P

MESH = pl.DeviceIdType.MESH
BF16, F32, I32 = jnp.bfloat16, jnp.float32, jnp.int32

IMG = 16
WIN = 17
ROWS = 56
IMGS = 14
HALF = IMGS * IMG
K = 4608
TILE = 128
UNITS = 5
SENDS = 160


def place(enc, tp):
    z_lo, rest = lax.div(enc, 8), lax.rem(enc, 8)
    return z_lo, lax.div(rest, 2), lax.rem(rest, 2), lax.div(tp, 4), lax.rem(tp, 4)


def device(z_lo, x, core, z_hi, y):
    return (z_lo * 8 + x * 2 + core, z_hi * 4 + y)


def running(values):
    count = values.shape[0]
    row = lax.broadcasted_iota(I32, values.shape, 0)
    total = values
    step = 1
    while step < count:
        total = total + jnp.where(row >= step, pltpu.roll(total, step, 0), 0)
        step *= 2
    return total - values


def exchange(
    vit, w, bias, seq, tokens,
    arrived, keys,
    held, weight, g0, g1, g2, g3, g4, staged, acc, joined, other_bias, table, lists, list_s,
    ssem, rsem, lsem, ws, wr, ls, lr, ds, dr,
):
    gathered = (g0, g1, g2, g3, g4)
    enc, tp = lax.axis_index("enc"), lax.axis_index("tp")
    z_lo, x, core, z_hi, y = place(enc, tp)
    z = z_hi * 4 + z_lo
    odd = lax.rem(x, 2)
    x_half = lax.div(x, 2)

    def at_xy(dx, dy):
        return device(z_lo, lax.rem(x + dx + 4, 4), core, z_hi, lax.rem(y + dy + 4, 4))

    def at_z(d):
        there = lax.rem(z + d + 8, 8)
        return device(lax.rem(there, 4), x, core, lax.div(there, 4), y)

    sibling = device(z_lo, x, 1 - core, z_hi, y)
    across = device(z_lo, x, core, 1 - z_hi, y)

    def at_lo(d):
        return device(lax.rem(z_lo + d, 4), x, core, z_hi, y)

    def scatter_to(b):
        return device(z_lo, 2 * z_hi + b, core, x_half, y)

    far = x_half != z_hi

    barrier = pltpu.get_barrier_semaphore()
    peers = [at_xy(d // 4, d % 4) for d in range(1, 16)]
    peers += [at_z(1), at_z(-1), sibling, across] + [at_lo(d) for d in (1, 2, 3)]
    for peer in peers:
        pl.semaphore_signal(barrier, inc=1, device_id=peer, device_id_type=MESH)

    @pl.when(far)
    def _():
        for b in range(2):
            pl.semaphore_signal(barrier, inc=1, device_id=scatter_to(b), device_id_type=MESH)

    pl.semaphore_wait(barrier, len(peers) + jnp.where(far, 2, 0))

    sends = []

    def put(src, dst, to):
        number = len(sends)
        copy = pltpu.make_async_remote_copy(
            src_ref=src, dst_ref=dst, send_sem=ssem.at[number], recv_sem=rsem.at[number],
            device_id=to, device_id_type=MESH,
        )
        copy.start()
        sends.append(copy)
        return number

    def got(number, dst):
        pltpu.make_async_remote_copy(
            src_ref=dst, dst_ref=dst, send_sem=ssem.at[number], recv_sem=rsem.at[number],
            device_id=sibling, device_id_type=MESH,
        ).wait_recv()

    part = K // 2

    def block(level, p, rx, ry, half=None):
        rows = pl.ds(0, 64) if level == 0 else pl.ds(64, 48)
        if half is None:
            return held.at[rx * 4 + ry, rows, pl.ds(p * part, part)]
        return held.at[rx * 4 + ry, rows, pl.ds(p * part + half * (part // 2), part // 2)]

    def near(p, first, second):
        return (second, first) if p == 0 else (first, second)

    def step_to(p, axis, d):
        return at_xy(*(near(p, d, 0) if axis == 0 else near(p, 0, d)))

    ids = {}

    def send_block(level, p, axis, d, first, second, half=None, src=None):
        if axis == 0:
            there = ((first - d) % 4, second)
        else:
            there = (first, (second - d) % 4)
        src = block(level, p, *near(p, first, second), half) if src is None else src
        ids[(level, p, there, half)] = put(
            src, block(level, p, *near(p, *there), half), step_to(p, axis, d)
        )

    def have(level, p, first, second, half=None):
        got(ids[(level, p, (first, second), half)], block(level, p, *near(p, first, second), half))

    def vit_own(level):
        rows = pl.ds(0, 64) if level == 0 else pl.ds(64, 48)
        for axis in range(2):
            for p in range(2):
                for d in (1, -1):
                    send_block(level, p, axis, d, 0, 0, src=vit.at[rows, pl.ds(p * part, part)])

    def vit_step(level, number):
        both = (0, 1)
        if number == 1:
            for p in both:
                for d in (1, -1):
                    off = (-d) % 4
                    have(level, p, off, 0)
                    send_block(level, p, 0, d, off, 0, half=0 if d == 1 else 1)
                    for d2 in (1, -1):
                        send_block(level, p, 1, d2, off, 0)
        if number == 2:
            for p in both:
                for d in (1, -1):
                    off = (-d) % 4
                    have(level, p, 0, off)
                    send_block(level, p, 1, d, 0, off, half=0 if d == 1 else 1)
        if number == 3:
            for p in both:
                for half in both:
                    have(level, p, 2, 0, half)
                for d2 in (1, -1):
                    send_block(level, p, 1, d2, 2, 0)
        if number == 4:
            for first in (3, 1):
                for p in both:
                    for d in (1, -1):
                        off = (-d) % 4
                        have(level, p, first, off)
                        send_block(level, p, 1, d, first, off, half=0 if d == 1 else 1)
        if number == 5:
            for p in both:
                for d in (1, -1):
                    off = (-d) % 4
                    have(level, p, 2, off)
                    send_block(level, p, 1, d, 2, off, half=0 if d == 1 else 1)
        if number == 6:
            for first in (0, 3, 1, 2):
                for p in both:
                    for half in both:
                        have(level, p, first, 2, half)

    def scatter_parts(b):
        mine = weight.at[z_lo * 2 + x_half, odd, core]
        return (
            (w.at[0, :, pl.ds(384 * b, 256)], mine.at[:, pl.ds(0, 256)]),
            (w.at[b, :, pl.ds(256, 128)], mine.at[:, pl.ds(256, 128)]),
            (w.at[1, :, pl.ds(384 * b, 256)], mine.at[:, pl.ds(384, 256)]),
        )

    def scatter_copy(b, i):
        src, dst = scatter_parts(b)[i]
        return pltpu.make_async_remote_copy(
            src_ref=src, dst_ref=dst, send_sem=ws.at[b, i], recv_sem=wr.at[odd, i],
            device_id=scatter_to(b), device_id_type=MESH,
        )

    def stays(b):
        return jnp.logical_and(2 * z_hi + b == x, jnp.logical_not(far))

    def weight_scatter():
        for b in range(2):
            @pl.when(stays(b))
            def _():
                for i, (src, dst) in enumerate(scatter_parts(b)):
                    pltpu.make_async_copy(src, dst, wr.at[odd, i]).start()

            @pl.when(jnp.logical_not(stays(b)))
            def _():
                for i in range(3):
                    scatter_copy(b, i).start()

    def rows_of(d, whose=None):
        there = lax.rem(z + d + 8, 8)
        index = lax.rem(there, 4) * 2 + lax.div(there, 4)
        return weight.at[index, :, core if whose is None else whose]

    wid = {}

    def ring_send(kind, store, view, d, up):
        to = at_z(1) if up else at_z(-1)
        there = d - 1 if up else d + 1
        if abs(there) == 4:
            piece = view(d, 0 if up else 1)
        else:
            piece = view(d, None)
        store[(kind, there)] = put(piece, piece, to)

    def weight_view(d, half):
        there = lax.rem(z + d + 8, 8)
        index = lax.rem(there, 4) * 2 + lax.div(there, 4)
        if half is None:
            return weight.at[index, :, core]
        return weight.at[index, half, core]

    def weight_step(number):
        if number == 0:
            for i in range(2):
                for k, cols in enumerate(((0, 256), (256, 128), (384, 256))):
                    landing = weight.at[z_lo * 2 + z_hi, i, core, :, pl.ds(*cols)]
                    pltpu.make_async_remote_copy(
                        src_ref=landing, dst_ref=landing, send_sem=ws.at[0, k], recv_sem=wr.at[i, k],
                        device_id=sibling, device_id_type=MESH,
                    ).wait_recv()
            for up in (True, False):
                ring_send("w", wid, weight_view, 0, up)
            wid[("s", 0)] = put(weight_view(0, None), weight_view(0, None), sibling)
        else:
            ring_step("w", wid, weight_view, number)
            if number == 4:
                for d in (0, -1, 1, -2, 2, -3, 3, 4):
                    got(wid[("s", d)], rows_of(d, 1 - core))

    def ring_step(kind, store, view, number):
        if number < 4:
            for d, up in ((-number, True), (number, False)):
                got(store[(kind, d)], view(d, None))
                ring_send(kind, store, view, d, up)
                store[("s", d)] = put(view(d, None), view(d, None), sibling)
        else:
            got(store[(kind, -4)], view(-4, 0))
            got(store[(kind, 4)], view(4, 1))
            store[("s", 4)] = put(view(4, None), view(4, None), sibling)

    def merged_view(g, d, half, whose):
        start = (whose * 8 + lax.rem(z + d + 8, 8)) * (4 * IMGS)
        if half is None:
            return g.at[pl.ds(start, 4 * IMGS)]
        return g.at[pl.ds(start + half * 2 * IMGS, 2 * IMGS)]

    gid = [dict() for _ in range(UNITS)]

    def unit_view(unit):
        return lambda d, half: merged_view(gathered[unit], d, half, core)

    def unit_step(unit, number):
        view = unit_view(unit)
        if number == 0:
            for up in (True, False):
                ring_send("g", gid[unit], view, 0, up)
            gid[unit][("s", 0)] = put(view(0, None), view(0, None), sibling)
        elif number < 5:
            ring_step("g", gid[unit], view, number)
        else:
            for d in (0, -1, 1, -2, 2, -3, 3, 4):
                got(gid[unit][("s", d)], merged_view(gathered[unit], d, None, 1 - core))

    def project(level, column, width, units, bias_row):
        def one(r, _):
            def chunk(k, _):
                rows = held[pl.ds(r * 4, 4), pl.ds(pl.multiple_of(level * 48, 16), 64),
                            pl.ds(pl.multiple_of(k * part, TILE), part)]
                cols = weight[pl.ds(k * 4, 4), :, :, :, column:column + width]
                product = jnp.dot(
                    rows.reshape(256, part), cols.reshape(part, width), preferred_element_type=F32
                )

                @pl.when(k == 0)
                def _():
                    acc[:, :width] = product

                @pl.when(k != 0)
                def _():
                    acc[:, :width] += product
                return 0

            lax.fori_loop(0, 2, chunk, 0)
            for ry in range(4):
                start = pl.multiple_of(lax.rem(y + ry, 4) * ROWS, 8)
                joined[pl.ds(start, ROWS), :width] = acc[
                    pl.ds(pl.multiple_of(ry * 64 + level * 8, 8), ROWS), :width
                ]
            start = ((core * 8 + z) * 4 + lax.rem(x + r, 4)) * IMGS
            for i, unit in enumerate(units):
                cols = slice(i * TILE, (i + 1) * TILE)
                gathered[unit][pl.ds(start, IMGS)] = (
                    joined[:, cols] + bias_row[:, cols]
                ).astype(BF16).reshape(IMGS, IMG, TILE)
            return 0

        lax.fori_loop(0, 4, one, 0)

    def bias_of(level, column, width):
        mine = jnp.where(far, other_bias[...], bias[...])
        row = jnp.where(level == 0, mine[0:1], mine[1:2])
        if column is None:
            return jnp.where(odd == 0, row[:, 0:width], row[:, 384:384 + width])
        return row[:, column:column + width]

    def window_send(unit):
        g = gathered[unit]

        def one(d, _):
            dx, dy = lax.div(d, 4), lax.rem(d, 4)
            there = lax.rem(x + dx, 4) * 4 + lax.rem(y + dy, 4)
            for k in range(WIN):
                staged[unit, d, k] = g[list_s[there, 0, k]]
            dst = arrived.at[x * 4 + y, :, :, pl.ds(unit * TILE, TILE)]

            @pl.when(d == 0)
            def _():
                pltpu.make_async_copy(staged.at[unit, d], dst, dr.at[unit, d]).start()

            @pl.when(d != 0)
            def _():
                pltpu.make_async_remote_copy(
                    src_ref=staged.at[unit, d], dst_ref=dst, send_sem=ds.at[unit, d], recv_sem=dr.at[unit, d],
                    device_id=at_xy(dx, dy), device_id_type=MESH,
                ).start()
            return 0

        lax.fori_loop(0, 16, one, 0)

    def window_wait(unit):
        dst0 = arrived.at[x * 4 + y, :, :, pl.ds(unit * TILE, TILE)]
        pltpu.make_async_copy(staged.at[unit, 0], dst0, dr.at[unit, 0]).wait()

        def one(d, _):
            dx, dy = lax.div(d, 4), lax.rem(d, 4)
            here = lax.rem(x - dx + 4, 4) * 4 + lax.rem(y - dy + 4, 4)
            copy = pltpu.make_async_remote_copy(
                src_ref=staged.at[unit, d], dst_ref=arrived.at[here, :, :, pl.ds(unit * TILE, TILE)],
                send_sem=ds.at[unit, d], recv_sem=dr.at[unit, d],
                device_id=at_xy(dx, dy), device_id_type=MESH,
            )
            copy.wait_send()
            copy.wait_recv()
            return 0

        lax.fori_loop(1, 16, one, 0)

    lane = lax.broadcasted_iota(I32, (32, 128), 1)
    sub = lax.broadcasted_iota(I32, (32, 128), 0)

    def own_table():
        ours = jnp.where(seq[...] == lax.div(lane, 2), 1, 0)
        second = jnp.where(sub >= 14, 1, 0)
        where = ((core * 8 + second * 4 + z_lo) * 4 + x) * 14 + sub - 14 * second
        pick = jnp.logical_and(ours == 1, running(ours) == lax.rem(lane, 2))
        row = jnp.sum(jnp.where(pick, where, 0), axis=0, keepdims=True)
        table[enc] = jnp.broadcast_to(row, (8, 128))

    def own_list():
        here = [tokens[pl.ds(tp * 2 + i, 1), :] for i in range(2)]
        slots = [lax.shift_right_arithmetic(row, 4) for row in here]
        total = jnp.zeros((1, 128), I32)
        picked = jnp.zeros((1, 128), I32)
        key = [jnp.zeros((1, 128), I32) for _ in range(2)]
        for rank in range(2):
            hit = [jnp.where(row == sub * 2 + rank, 1, 0) for row in slots]
            present = jnp.max(jnp.maximum(hit[0], hit[1]), axis=1, keepdims=True)
            present = jnp.broadcast_to(present, (32, 128))
            position = running(present) + total
            total = total + jnp.sum(present, axis=0, keepdims=True)
            places = jnp.where(lane == enc * 2 + rank, table[:, 0, :], 0)
            places = jnp.sum(places, axis=1, keepdims=True)
            chosen = jnp.logical_and(present == 1, position == lane)
            picked = picked + jnp.sum(jnp.where(chosen, places, 0), axis=0, keepdims=True)
            for i in range(2):
                key[i] = key[i] + jnp.sum(hit[i] * position, axis=0, keepdims=True)
        lists[x * 4 + y] = jnp.broadcast_to(picked, (8, 128))
        for i in range(2):
            keys[i:i + 1, :] = jnp.where(here[i] < 0, -1, key[i] * IMG + jnp.bitwise_and(here[i], IMG - 1))

    def list_copy(d, back):
        dx, dy = lax.div(d, 4), lax.rem(d, 4)
        sign = -1 if back else 1
        slot = lax.rem(x - dx + 4, 4) * 4 + lax.rem(y - dy + 4, 4) if back else x * 4 + y
        return pltpu.make_async_remote_copy(
            src_ref=lists.at[x * 4 + y], dst_ref=lists.at[slot], send_sem=ls.at[d], recv_sem=lr.at[d],
            device_id=at_xy(dx, dy), device_id_type=MESH,
        )

    def list_send():
        def one(d, _):
            list_copy(d, False).start()
            return 0
        lax.fori_loop(1, 16, one, 0)

    def list_wait():
        def one(d, _):
            copy = list_copy(d, True)
            copy.wait_send()
            copy.wait_recv()
            return 0
        lax.fori_loop(1, 16, one, 0)
        copy = pltpu.make_async_copy(lists, list_s, lsem.at[1])
        copy.start()
        copy.wait()

    vit_own(0)
    mine = pltpu.make_async_copy(vit, held.at[0], lsem.at[0])
    mine.start()
    weight_scatter()
    bias_id = put(bias, other_bias, across)
    own_table()
    own = table.at[enc]
    sib_id = put(own, own, sibling)
    vit_step(0, 1)
    weight_step(0)
    got(sib_id, table.at[z_lo * 8 + x * 2 + 1 - core])
    pair = table.at[pl.ds(z_lo * 8 + x * 2, 2)]
    pair_ids = [put(pair, pair, at_xy(d, 0)) for d in (1, 2, 3)]
    vit_step(0, 2)
    for d, number in zip((1, 2, 3), pair_ids):
        got(number, table.at[pl.ds(z_lo * 8 + lax.rem(x - d + 4, 4) * 2, 2)])
    eight = table.at[pl.ds(z_lo * 8, 8)]
    lo_ids = [put(eight, eight, at_lo(d)) for d in (1, 2, 3)]
    weight_step(1)
    vit_step(0, 3)
    for d, number in zip((1, 2, 3), lo_ids):
        got(number, table.at[pl.ds(lax.rem(z_lo - d + 4, 4) * 8, 8)])
    own_list()
    list_send()
    weight_step(2)
    vit_step(0, 4)
    vit_own(1)
    weight_step(3)
    vit_step(0, 5)
    list_wait()
    got(bias_id, other_bias)
    weight_step(4)
    mine.wait()
    vit_step(0, 6)
    project(0, 0, 256, (0, 1), bias_of(0, None, 256))
    unit_step(0, 0)
    unit_step(1, 0)
    vit_step(1, 1)
    unit_step(0, 1)
    vit_step(1, 2)
    unit_step(1, 1)
    vit_step(1, 3)
    unit_step(0, 2)
    vit_step(1, 4)
    unit_step(1, 2)
    vit_step(1, 5)
    unit_step(0, 3)
    unit_step(1, 3)
    vit_step(1, 6)
    project(odd, 256, 128, (2,), bias_of(odd, 256, 128))
    unit_step(2, 0)
    project(1, 384, 256, (3, 4), bias_of(1, None, 256))
    unit_step(3, 0)
    unit_step(0, 4)
    unit_step(1, 4)
    unit_step(0, 5)
    unit_step(2, 1)
    window_send(0)
    unit_step(3, 1)
    unit_step(2, 2)
    unit_step(1, 5)
    window_send(1)
    unit_step(3, 2)
    unit_step(4, 0)
    unit_step(2, 3)
    unit_step(3, 3)
    unit_step(4, 1)
    unit_step(2, 4)
    unit_step(3, 4)
    unit_step(4, 2)
    unit_step(2, 5)
    window_send(2)
    unit_step(3, 5)
    window_send(3)
    unit_step(4, 3)
    unit_step(4, 4)
    unit_step(4, 5)
    window_send(4)
    for unit in range(UNITS):
        window_wait(unit)
    for copy in sends:
        copy.wait_send()
    for b in range(2):
        @pl.when(jnp.logical_not(stays(b)))
        def _():
            for i in range(3):
                scatter_copy(b, i).wait_send()


def finish(keys, arrived, residual, gain, out):
    level = pl.program_id(0)
    tokens = residual.shape[1]
    key = jnp.concatenate([keys[0:1, :], keys[1:2, :]], axis=1)
    hot = jnp.where(lax.broadcasted_iota(I32, (WIN * IMG, tokens), 0) == key, 1.0, 0.0).astype(BF16)

    def for_level(lvl):
        square = jnp.zeros((tokens, TILE), F32)

        def add(start, source, column, width, square):
            rows = arrived[source, :, :, column:column + width].reshape(WIN * IMG, width)
            deep = lax.dot_general(
                hot, rows, (((0,), (0,)), ((), ())),
                preferred_element_type=F32,
            )
            total = (residual[0, :, start:start + width].astype(F32) + deep).astype(BF16)
            out[0, :, start:start + width] = total
            total = total.astype(F32)
            for i in range(0, width, TILE):
                piece = total[:, i:i + TILE]
                square = square + piece * piece
            return square

        for source in range(16):
            sx, sy = source // 4, source % 4
            base = ((sx // 2) * 4 + sy) * 640
            square = add(base + 384 * (sx % 2), source, 0 if lvl == 0 else 384, 256, square)
            if sx % 2 == lvl:
                square = add(base + 256, source, 256, 128, square)
        mean = jnp.sum(square, axis=1, keepdims=True) * (1.0 / 5120)
        scale = lax.rsqrt(mean + 1e-06)
        for start in range(0, 5120, 512):
            cols = slice(start, start + 512)
            values = out[0, :, cols].astype(F32)
            out[0, :, cols] = (values * scale * gain[lvl:lvl + 1, cols].astype(F32)).astype(BF16)

    @pl.when(level == 0)
    def _():
        for_level(0)

    @pl.when(level == 1)
    def _():
        for_level(1)


def per_device(
    vit_hidden, merge_weight, merge_bias, residual, norm_gain, image_sequence, token_source
):
    vit = vit_hidden.reshape(2 * ROWS, K)
    bias = jnp.pad(merge_bias.astype(F32), ((0, 6), (0, 0)))
    seq = jnp.broadcast_to(jnp.pad(image_sequence, (0, 4), constant_values=-1)[:, None], (32, 128))
    tokens = token_source.reshape(16, 128)
    any_, vmem = pl.BlockSpec(memory_space=pl.ANY), pl.BlockSpec(memory_space=pltpu.VMEM)
    arrived, keys = pl.pallas_call(
        exchange,
        name="exchange",
        out_shape=(
            jax.ShapeDtypeStruct((16, WIN, IMG, UNITS * TILE), BF16),
            jax.ShapeDtypeStruct((8, 128), I32),
        ),
        in_specs=[any_, any_, vmem, vmem, vmem],
        out_specs=(any_, vmem),
        scratch_shapes=[
            pltpu.VMEM((16, 2 * ROWS, K), BF16),
            pltpu.VMEM((8, 2, 2, 144, UNITS * TILE), BF16),
        ]
        + [pltpu.VMEM((64 * IMGS, IMG, TILE), BF16)] * UNITS
        + [
            pltpu.VMEM((UNITS, 16, WIN, IMG, TILE), BF16),
            pltpu.VMEM((256, 256), F32),
            pltpu.VMEM((HALF, 256), F32),
            pltpu.VMEM((8, 640), F32),
            pltpu.VMEM((32, 8, 128), I32),
            pltpu.VMEM((16, 8, 128), I32),
            pltpu.SMEM((16, 8, 128), I32),
            pltpu.SemaphoreType.DMA((SENDS + 40,)),
            pltpu.SemaphoreType.DMA((SENDS + 40,)),
            pltpu.SemaphoreType.DMA((2,)),
            pltpu.SemaphoreType.DMA((2, 3)),
            pltpu.SemaphoreType.DMA((2, 3)),
            pltpu.SemaphoreType.DMA((16,)),
            pltpu.SemaphoreType.DMA((16,)),
            pltpu.SemaphoreType.DMA((UNITS, 16)),
            pltpu.SemaphoreType.DMA((UNITS, 16)),
        ],
        compiler_params=pltpu.CompilerParams(
            collective_id=0, has_side_effects=True, vmem_limit_bytes=60 << 20
        ),
        cost_estimate=pl.CostEstimate(
            flops=2 * 2 * 448 * K * 640, bytes_accessed=8 << 20, transcendentals=0
        ),
    )(vit, merge_weight, bias, seq, tokens)
    count = residual.shape[1]
    return pl.pallas_call(
        finish,
        name="finish",
        grid=(2,),
        out_shape=jax.ShapeDtypeStruct(residual.shape, BF16),
        in_specs=[
            pl.BlockSpec((8, 128), lambda i: (0, 0)),
            pl.BlockSpec((16, WIN, IMG, UNITS * TILE), lambda i: (0, 0, 0, 0)),
            pl.BlockSpec((1, count, 5120), lambda i: (i, 0, 0)),
            pl.BlockSpec((2, 5120), lambda i: (0, 0)),
        ],
        out_specs=pl.BlockSpec((1, count, 5120), lambda i: (i, 0, 0)),
        compiler_params=pltpu.CompilerParams(vmem_limit_bytes=48 << 20),
    )(keys, arrived, residual, norm_gain)


def solution(mesh):
    return jax.shard_map(
        per_device,
        mesh=mesh,
        in_specs=(
            P(None, ("enc", "tp"), None),
            P(None, "enc", "tp"),
            P(None, "tp"),
            P(None, ("enc", "tp"), None),
            P(),
            P("enc"),
            P("enc"),
        ),
        out_specs=P(None, ("enc", "tp"), None),
        check_vma=False,
    )
```

```python
import functools

import jax
import jax.numpy as jnp
from jax import lax
from jax.experimental import pallas as pl
from jax.experimental.pallas import tpu as pltpu
from jax.sharding import PartitionSpec as P

MESH = pl.DeviceIdType.MESH
BF16, F32, I32 = jnp.bfloat16, jnp.float32, jnp.int32

IMG = 16
WIN = 17
ROWS = 56
IMGS = 14
HALF = IMGS * IMG
K = 4608
TILE = 128
UNITS = 5
SENDS = 300


def place(enc, tp):
    z_lo, rest = lax.div(enc, 8), lax.rem(enc, 8)
    return z_lo, lax.div(rest, 2), lax.rem(rest, 2), lax.div(tp, 4), lax.rem(tp, 4)


def device(z_lo, x, core, z_hi, y):
    return (z_lo * 8 + x * 2 + core, z_hi * 4 + y)


def running(values):
    count = values.shape[0]
    row = lax.broadcasted_iota(I32, values.shape, 0)
    total = values
    step = 1
    while step < count:
        total = total + jnp.where(row >= step, pltpu.roll(total, step, 0), 0)
        step *= 2
    return total - values


def exchange(
    vit, w, bias, images, tokens,
    arrived, keys,
    held, weight, g0, g1, g2, g3, g4, staged, acc, joined, own_bias, other_bias, table, lists, list_s,
    ssem, rsem, lsem, ws, wr, ls, lr, ds, dr,
):
    gathered = (g0, g1, g2, g3, g4)
    enc, tp = lax.axis_index("enc"), lax.axis_index("tp")
    z_lo, x, core, z_hi, y = place(enc, tp)
    z = z_hi * 4 + z_lo
    odd = lax.rem(x, 2)
    x_half = lax.div(x, 2)

    def at_xy(dx, dy):
        return device(z_lo, lax.rem(x + dx + 4, 4), core, z_hi, lax.rem(y + dy + 4, 4))

    def at_z(d):
        there = lax.rem(z + d + 8, 8)
        return device(lax.rem(there, 4), x, core, lax.div(there, 4), y)

    sibling = device(z_lo, x, 1 - core, z_hi, y)
    across = device(z_lo, x, core, 1 - z_hi, y)

    def at_lo(d):
        return device(lax.rem(z_lo + d, 4), x, core, z_hi, y)

    def scatter_to(b, i):
        side = 1 - z_hi if i == 2 else z_hi
        return device(z_lo, 2 * side + b, core, x_half, y)

    far = x_half != z_hi

    barrier = pltpu.get_barrier_semaphore()
    peers = [at_xy(d // 4, d % 4) for d in range(1, 16)]
    peers += [at_z(1), at_z(-1), sibling, across] + [at_lo(d) for d in (1, 2, 3)]
    senders = [device(z_lo, 2 * z_hi + i, core, 1 - z_hi, y) for i in range(2)]
    for peer in peers + senders:
        pl.semaphore_signal(barrier, inc=1, device_id=peer, device_id_type=MESH)
    pl.semaphore_wait(barrier, len(peers) + jnp.where(far, 4, 0))

    sends = {}

    def descriptor(key):
        number, like = sends[key]
        return pltpu.make_async_remote_copy(
            src_ref=like(), dst_ref=like(), send_sem=ssem.at[number], recv_sem=rsem.at[number],
            device_id=sibling, device_id_type=MESH,
        )

    def put(key, src, like, to, dst=None):
        number = sends.setdefault(key, (len(sends), like))[0]
        pltpu.make_async_remote_copy(
            src_ref=src, dst_ref=like() if dst is None else dst, send_sem=ssem.at[number],
            recv_sem=rsem.at[number], device_id=to, device_id_type=MESH,
        ).start()

    def got(key, dst):
        number = sends[key][0]
        pltpu.make_async_remote_copy(
            src_ref=dst, dst_ref=dst, send_sem=ssem.at[number], recv_sem=rsem.at[number],
            device_id=sibling, device_id_type=MESH,
        ).wait_recv()

    part = K // 2

    def block(level, p, rx, ry, half=None):
        rows = pl.ds(0, 64) if level == 0 else pl.ds(64, 48)
        if half is None:
            return held.at[rx * 4 + ry, rows, pl.ds(p * part, part)]
        return held.at[rx * 4 + ry, rows, pl.ds(p * part + half * (part // 2), part // 2)]

    def near(p, first, second):
        return (second, first) if p == 0 else (first, second)

    def step_to(p, axis, d):
        return at_xy(*(near(p, d, 0) if axis == 0 else near(p, 0, d)))

    def send_block(level, p, axis, d, first, second, half=None, src=None):
        if axis == 0:
            there = ((first - d) % 4, second)
        else:
            there = (first, (second - d) % 4)
        src = block(level, p, *near(p, first, second), half) if src is None else src
        put(("v", level, p, there, half), src, lambda: block(level, p, *near(p, *there), half), step_to(p, axis, d))

    def have(level, p, first, second, half=None):
        got(("v", level, p, (first, second), half), block(level, p, *near(p, first, second), half))

    def vit_own(level, ways=((0, 0), (0, 1), (1, 0), (1, 1))):
        rows = pl.ds(0, 64) if level == 0 else pl.ds(64, 48)
        for axis, p in ways:
            if True:
                for d in (1, -1):
                    send_block(level, p, axis, d, 0, 0, src=vit.at[rows, pl.ds(p * part, part)])

    def vit_step(level, number):
        both = (0, 1)
        if number == 1:
            for p in both:
                for d in (1, -1):
                    off = (-d) % 4
                    have(level, p, off, 0)
                    send_block(level, p, 0, d, off, 0, half=0 if d == 1 else 1)
                    for d2 in (1, -1):
                        send_block(level, p, 1, d2, off, 0)
        if number == 2:
            for p in both:
                for d in (1, -1):
                    off = (-d) % 4
                    have(level, p, 0, off)
                    send_block(level, p, 1, d, 0, off, half=0 if d == 1 else 1)
        if number == 3:
            for p in both:
                for half in both:
                    have(level, p, 2, 0, half)
                for d2 in (1, -1):
                    send_block(level, p, 1, d2, 2, 0)
        if number in (4, 5):
            for first in ((3,) if number == 4 else (1,)):
                for p in both:
                    for d in (1, -1):
                        off = (-d) % 4
                        have(level, p, first, off)
                        send_block(level, p, 1, d, first, off, half=0 if d == 1 else 1)
        if number == 6:
            for p in both:
                for d in (1, -1):
                    off = (-d) % 4
                    have(level, p, 2, off)
                    send_block(level, p, 1, d, 2, off, half=0 if d == 1 else 1)
        if number in (7, 8):
            for first in ((0,) if number == 7 else (3, 1, 2)):
                for p in both:
                    for half in both:
                        have(level, p, first, 2, half)

    def scatter_parts(b):
        mine = weight.at[z_lo * 2 + x_half, odd, core]
        return (
            (w.at[0, :, pl.ds(384 * b, 256)], mine.at[:, pl.ds(0, 256)]),
            (w.at[b, :, pl.ds(256, 128)], mine.at[:, pl.ds(256, 128)]),
            (w.at[1, :, pl.ds(384 * b, 256)], mine.at[:, pl.ds(384, 256)]),
        )

    def scatter_copy(b, i):
        src, dst = scatter_parts(b)[i]
        return pltpu.make_async_remote_copy(
            src_ref=src, dst_ref=dst, send_sem=ws.at[b, i], recv_sem=wr.at[odd, i],
            device_id=scatter_to(b, i), device_id_type=MESH,
        )

    def stays(b):
        return jnp.logical_and(2 * z_hi + b == x, jnp.logical_not(far))

    def weight_scatter():
        for b in range(2):
            @pl.when(stays(b))
            def _():
                for i, (src, dst) in enumerate(scatter_parts(b)[:2]):
                    pltpu.make_async_copy(src, dst, wr.at[odd, i]).start()

            @pl.when(jnp.logical_not(stays(b)))
            def _():
                for i in range(2):
                    scatter_copy(b, i).start()
        for b in range(2):
            scatter_copy(b, 2).start()

    wide = ((0, 384), (384, 256))

    def ring_send(kind, view, d, up):
        to = at_z(1) if up else at_z(-1)
        there = d - 1 if up else d + 1
        half = None if abs(there) < 4 else 0 if up else 1
        put((kind, there), view(d, half), lambda: view(d, half), to)

    def core_send(kind, view, d):
        put((kind, "core", d), view(d, None), lambda: view(d, None), sibling)

    def weight_view(part_, whose):
        cols = pl.ds(*wide[part_])

        def view(d, half):
            there = lax.rem(z + d + 8, 8)
            index = lax.rem(there, 4) * 2 + lax.div(there, 4)
            if half is None:
                return weight.at[index, :, whose, :, cols]
            return weight.at[index, half, whose, :, cols]
        return view

    def weight_step(part_, number):
        view = weight_view(part_, core)
        kind = ("w", part_)
        if number == 0:
            for i in range(2):
                for k, cols in (((0, (0, 256)), (1, (256, 128))), ((2, (384, 256)),))[part_]:
                    landing = weight.at[z_lo * 2 + z_hi, i, core, :, pl.ds(*cols)]
                    pltpu.make_async_remote_copy(
                        src_ref=landing, dst_ref=landing, send_sem=ws.at[0, k], recv_sem=wr.at[i, k],
                        device_id=sibling, device_id_type=MESH,
                    ).wait_recv()
            for up in (True, False):
                ring_send(kind, view, 0, up)
            core_send(kind, view, 0)
        elif number < 5:
            ring_step(kind, view, number)
        else:
            for d in (0, -1, 1, -2, 2, -3, 3, 4):
                got((kind, "core", d), weight_view(part_, 1 - core)(d, None))

    def ring_step(kind, view, number):
        if number < 4:
            for d, up in ((-number, True), (number, False)):
                got((kind, d), view(d, None))
                ring_send(kind, view, d, up)
                core_send(kind, view, d)
        else:
            got((kind, -4), view(-4, 0))
            got((kind, 4), view(4, 1))
            core_send(kind, view, 4)

    def merged_view(g, group, d, half, whose):
        count = IMGS if group == 0 else 3 * IMGS
        start = (whose * 8 + lax.rem(z + d + 8, 8)) * (4 * IMGS) + group * IMGS
        if half is None:
            return g.at[pl.ds(start, count)]
        return g.at[pl.ds(start + half * (count // 2), count // 2)]

    def unit_step(unit, group, number):
        kind = ("g", unit, group)

        def view(d, half):
            return merged_view(gathered[unit], group, d, half, core)

        if number == 0:
            for up in (True, False):
                ring_send(kind, view, 0, up)
            core_send(kind, view, 0)
        elif number < 5:
            ring_step(kind, view, number)
        else:
            for d in (0, -1, 1, -2, 2, -3, 3, 4):
                got((kind, "core", d), merged_view(gathered[unit], group, d, None, 1 - core))

    def project(group, level, column, width, units, bias_row):
        def one(r, _):
            def chunk(k, _):
                rows = held[pl.ds(r * 4, 4), pl.ds(pl.multiple_of(level * 48, 16), 64),
                            pl.ds(pl.multiple_of(k * part, TILE), part)]
                cols = weight[pl.ds(k * 4, 4), :, :, :, column:column + width]
                product = jnp.dot(
                    rows.reshape(256, part), cols.reshape(part, width), preferred_element_type=F32
                )

                @pl.when(k == 0)
                def _():
                    acc[:, :width] = product

                @pl.when(k != 0)
                def _():
                    acc[:, :width] += product
                return 0

            lax.fori_loop(0, 2, chunk, 0)
            for ry in range(4):
                start = pl.multiple_of(lax.rem(y + ry, 4) * ROWS, 8)
                joined[pl.ds(start, ROWS), :width] = acc[
                    pl.ds(pl.multiple_of(ry * 64 + level * 8, 8), ROWS), :width
                ]
            start = ((core * 8 + z) * 4 + r) * IMGS
            for i, unit in enumerate(units):
                cols = slice(i * TILE, (i + 1) * TILE)
                gathered[unit][pl.ds(start, IMGS)] = (
                    joined[:, cols] + bias_row[:, cols]
                ).astype(BF16).reshape(IMGS, IMG, TILE)
            return 0

        lax.fori_loop(*((0, 1) if group == 0 else (1, 4)), one, 0)

    def bias_of(level, column, width):
        mine = jnp.where(jnp.logical_xor(far, column is None and level == 1), other_bias[...], own_bias[...])
        row = jnp.where(level == 0, mine[0:1], mine[1:2])
        if column is None:
            return jnp.where(odd == 0, row[:, 0:width], row[:, 384:384 + width])
        return row[:, column:column + width]

    def window_send(unit):
        g = gathered[unit]

        def one(d, _):
            dx, dy = lax.div(d, 4), lax.rem(d, 4)
            there = lax.rem(x + dx, 4) * 4 + lax.rem(y + dy, 4)
            for k in range(WIN):
                staged[unit, d, k] = g[list_s[there, 0, k]]
            dst = arrived.at[x * 4 + y, :, :, pl.ds(unit * TILE, TILE)]

            @pl.when(d == 0)
            def _():
                pltpu.make_async_copy(staged.at[unit, d], dst, dr.at[unit, d]).start()

            @pl.when(d != 0)
            def _():
                pltpu.make_async_remote_copy(
                    src_ref=staged.at[unit, d], dst_ref=dst, send_sem=ds.at[unit, d], recv_sem=dr.at[unit, d],
                    device_id=at_xy(dx, dy), device_id_type=MESH,
                ).start()
            return 0

        lax.fori_loop(0, 16, one, 0)

    def window_wait(unit):
        dst0 = arrived.at[x * 4 + y, :, :, pl.ds(unit * TILE, TILE)]
        pltpu.make_async_copy(staged.at[unit, 0], dst0, dr.at[unit, 0]).wait()

        def one(d, _):
            dx, dy = lax.div(d, 4), lax.rem(d, 4)
            here = lax.rem(x - dx + 4, 4) * 4 + lax.rem(y - dy + 4, 4)
            copy = pltpu.make_async_remote_copy(
                src_ref=staged.at[unit, d], dst_ref=arrived.at[here, :, :, pl.ds(unit * TILE, TILE)],
                send_sem=ds.at[unit, d], recv_sem=dr.at[unit, d],
                device_id=at_xy(dx, dy), device_id_type=MESH,
            )
            copy.wait_send()
            copy.wait_recv()
            return 0

        lax.fori_loop(1, 16, one, 0)

    lane = lax.broadcasted_iota(I32, (32, 128), 1)
    sub = lax.broadcasted_iota(I32, (32, 128), 0)

    def own_table():
        of = jnp.full((32, 128), -1, I32)
        for i in range(2 * IMGS):
            of = jnp.where(sub == i, images[i], of)
        ours = jnp.where(of == lax.div(lane, 2), 1, 0)
        second = jnp.where(sub >= 14, 1, 0)
        where = ((core * 8 + second * 4 + z_lo) * 16 + sub - IMGS * second) * 4 + x
        pick = jnp.logical_and(ours == 1, running(ours) == lax.rem(lane, 2))
        row = jnp.sum(jnp.where(pick, where, 0), axis=0, keepdims=True)
        table[enc] = jnp.broadcast_to(row, (8, 128))

    def own_list():
        here = [tokens[pl.ds(tp * 2 + i, 1), :] for i in range(2)]
        slots = [lax.shift_right_arithmetic(row, 4) for row in here]
        total = jnp.zeros((1, 128), I32)
        picked = jnp.zeros((1, 128), I32)
        key = [jnp.zeros((1, 128), I32) for _ in range(2)]
        for rank in range(2):
            hit = [jnp.where(row == sub * 2 + rank, 1, 0) for row in slots]
            present = jnp.max(jnp.maximum(hit[0], hit[1]), axis=1, keepdims=True)
            present = jnp.broadcast_to(present, (32, 128))
            position = running(present) + total
            total = total + jnp.sum(present, axis=0, keepdims=True)
            places = jnp.where(lane == enc * 2 + rank, table[:, 0, :], 0)
            places = jnp.sum(places, axis=1, keepdims=True)
            chosen = jnp.logical_and(present == 1, position == lane)
            picked = picked + jnp.sum(jnp.where(chosen, places, 0), axis=0, keepdims=True)
            for i in range(2):
                key[i] = key[i] + jnp.sum(hit[i] * position, axis=0, keepdims=True)
        lists[x * 4 + y] = jnp.broadcast_to(picked, (8, 128))
        for i in range(2):
            keys[i:i + 1, :] = jnp.where(here[i] < 0, -1, key[i] * IMG + jnp.bitwise_and(here[i], IMG - 1))

    def list_copy(d, back):
        dx, dy = lax.div(d, 4), lax.rem(d, 4)
        sign = -1 if back else 1
        slot = lax.rem(x - dx + 4, 4) * 4 + lax.rem(y - dy + 4, 4) if back else x * 4 + y
        return pltpu.make_async_remote_copy(
            src_ref=lists.at[x * 4 + y], dst_ref=lists.at[slot], send_sem=ls.at[d], recv_sem=lr.at[d],
            device_id=at_xy(dx, dy), device_id_type=MESH,
        )

    def list_send():
        def one(d, _):
            list_copy(d, False).start()
            return 0
        lax.fori_loop(1, 16, one, 0)

    def list_wait():
        def one(d, _):
            copy = list_copy(d, True)
            copy.wait_send()
            copy.wait_recv()
            return 0
        lax.fori_loop(1, 16, one, 0)
        value = lists[...]
        r = jnp.bitwise_and(jnp.bitwise_and(value, 3) + (4 - x), 3)
        image = jnp.bitwise_and(lax.shift_right_logical(value, 2), 15)
        lists[...] = (lax.shift_right_logical(value, 6) * 4 + r) * IMGS + image
        copy = pltpu.make_async_copy(lists, list_s, lsem.at[1])
        copy.start()
        copy.wait()

    weight_scatter()
    vit_own(0)
    mine = pltpu.make_async_copy(vit, held.at[0], lsem.at[0])
    mine.start()
    own_table()
    own_bias[...] = jnp.zeros((8, 640), F32)
    own_bias[0:2, :] = bias[...].astype(F32)
    own = table.at[enc]
    put("one", own, lambda: own, sibling)
    put("bias", own_bias, lambda: other_bias, across)
    vit_step(0, 1)
    weight_step(0, 0)
    weight_step(1, 0)
    vit_step(0, 2)
    got("one", table.at[z_lo * 8 + x * 2 + 1 - core])
    pair = table.at[pl.ds(z_lo * 8 + x * 2, 2)]
    for d in (1, 2, 3):
        put(("pair", d), pair, lambda: pair, at_xy(d, 0))
    weight_step(0, 1)
    weight_step(1, 1)
    weight_step(0, 2)
    vit_step(0, 3)
    vit_step(0, 4)
    vit_step(0, 5)
    weight_step(1, 2)
    weight_step(0, 3)
    vit_step(0, 7)
    weight_step(1, 3)
    for d in (1, 2, 3):
        got(("pair", d), table.at[pl.ds(z_lo * 8 + lax.rem(x - d + 4, 4) * 2, 2)])
    eight = table.at[pl.ds(z_lo * 8, 8)]
    for d in (1, 2, 3):
        put(("eight", d), eight, lambda: eight, at_lo(d))
    weight_step(0, 4)
    vit_step(0, 6)
    vit_own(1)
    weight_step(1, 4)
    weight_step(0, 5)
    weight_step(1, 5)
    mine.wait()
    got("bias", other_bias)
    a = (0, 0, 256, (0, 1), bias_of(0, None, 256))
    project(0, *a)
    unit_step(0, 0, 0)
    unit_step(1, 0, 0)
    unit_step(0, 0, 1)
    unit_step(1, 0, 1)
    vit_step(0, 8)
    project(1, *a)
    unit_step(0, 1, 0)
    unit_step(1, 1, 0)
    unit_step(0, 0, 2)
    unit_step(1, 0, 2)
    for d in (1, 2, 3):
        got(("eight", d), table.at[pl.ds(lax.rem(z_lo - d + 4, 4) * 8, 8)])
    own_list()
    list_send()

    def window(unit):
        unit_step(unit, 0, 5)
        unit_step(unit, 1, 5)
        window_send(unit)

    def rest(even):
        b = (0 if even else 1, 256, 128, (2,), bias_of(0 if even else 1, 256, 128))
        c = (1, 384, 256, (3, 4), bias_of(1, None, 256))
        few = (3, 4) if even else (2, 3, 4)

        def small(number):
            for unit in few:
                unit_step(unit, 0, number)

        vit_step(1, 1)
        vit_step(1, 2)
        if even:
            project(0, *b)
            project(1, *b)
        unit_step(0, 0, 3)
        unit_step(1, 0, 3)
        unit_step(0, 1, 1)
        unit_step(1, 1, 1)
        unit_step(0, 0, 4)
        unit_step(1, 0, 4)
        if even:
            unit_step(2, 0, 0)
            unit_step(2, 1, 0)
        unit_step(0, 1, 2)
        vit_step(1, 3)
        unit_step(1, 1, 2)
        vit_step(1, 7)
        vit_step(1, 4)
        vit_step(1, 5)
        if not even:
            project(0, *b)
            unit_step(2, 0, 0)
        project(0, *c)
        unit_step(3, 0, 0)
        unit_step(4, 0, 0)
        unit_step(0, 1, 3)
        vit_step(1, 6)
        unit_step(1, 1, 3)
        unit_step(0, 1, 4)
        list_wait()
        window(0)
        vit_step(1, 8)
        if even:
            project(1, *c)
            unit_step(3, 1, 0)
            unit_step(1, 1, 4)
            window(1)
            unit_step(2, 0, 1)
            unit_step(2, 1, 1)
            small(1)
            unit_step(2, 0, 2)
            unit_step(2, 1, 2)
            unit_step(3, 1, 1)
            small(2)
            unit_step(2, 0, 3)
            unit_step(2, 1, 3)
            unit_step(3, 1, 2)
            unit_step(4, 1, 0)
            small(3)
            unit_step(2, 0, 4)
            unit_step(2, 1, 4)
            window(2)
            small(4)
        else:
            project(1, *b)
            unit_step(2, 1, 0)
            unit_step(1, 1, 4)
            window(1)
            small(1)
            project(1, *c)
            unit_step(2, 1, 1)
            small(2)
            unit_step(2, 1, 2)
            unit_step(3, 1, 0)
            small(3)
            unit_step(2, 1, 3)
            small(4)
            unit_step(3, 1, 1)
            unit_step(2, 1, 4)
            unit_step(4, 1, 0)
            window(2)
            unit_step(3, 1, 2)
        unit_step(3, 1, 3)
        unit_step(4, 1, 1)
        unit_step(3, 1, 4)
        window(3)
        unit_step(4, 1, 2)
        unit_step(4, 1, 3)
        unit_step(4, 1, 4)
        window(4)

    @pl.when(odd == 0)
    def _():
        rest(True)

    @pl.when(odd == 1)
    def _():
        rest(False)

    for unit in range(UNITS):
        window_wait(unit)
    for key in sends:
        descriptor(key).wait_send()
    for b in range(2):
        @pl.when(jnp.logical_not(stays(b)))
        def _():
            for i in range(2):
                scatter_copy(b, i).wait_send()
        scatter_copy(b, 2).wait_send()


def finish(keys, arrived, residual, gain, out):
    level = pl.program_id(0)
    tokens = residual.shape[1]
    key = keys[pl.ds(pl.program_id(1), 1), :]
    hot = jnp.where(lax.broadcasted_iota(I32, (WIN * IMG, tokens), 0) == key, 1.0, 0.0).astype(BF16)

    def for_level(lvl):
        square = jnp.zeros((tokens, TILE), F32)

        def add(start, source, column, width, square):
            rows = arrived[source, :, :, column:column + width].reshape(WIN * IMG, width)
            deep = lax.dot_general(
                hot, rows, (((0,), (0,)), ((), ())),
                preferred_element_type=F32,
            )
            total = (residual[0, :, start:start + width].astype(F32) + deep).astype(BF16)
            out[0, :, start:start + width] = total
            total = total.astype(F32)
            for i in range(0, width, TILE):
                piece = total[:, i:i + TILE]
                square = square + piece * piece
            return square

        for source in range(16):
            sx, sy = source // 4, source % 4
            base = ((sx // 2) * 4 + sy) * 640
            other = ((1 - sx // 2) * 4 + sy) * 640
            if lvl == 0:
                square = add(base + 384 * (sx % 2), source, 0, 256, square)
            else:
                square = add(other + 384 * (sx % 2), source, 384, 256, square)
            if sx % 2 == lvl:
                square = add(base + 256, source, 256, 128, square)
        mean = jnp.sum(square, axis=1, keepdims=True) * (1.0 / 5120)
        scale = lax.rsqrt(mean + 1e-06)
        for start in range(0, 5120, 512):
            cols = slice(start, start + 512)
            values = out[0, :, cols].astype(F32)
            out[0, :, cols] = (values * scale * gain[lvl:lvl + 1, cols].astype(F32)).astype(BF16)

    @pl.when(level == 0)
    def _():
        for_level(0)

    @pl.when(level == 1)
    def _():
        for_level(1)


def per_device(
    vit_hidden, merge_weight, merge_bias, residual, norm_gain, image_sequence, token_source
):
    vit = vit_hidden.reshape(2 * ROWS, K)
    tokens = token_source.reshape(16, 128)
    any_, vmem = pl.BlockSpec(memory_space=pl.ANY), pl.BlockSpec(memory_space=pltpu.VMEM)
    arrived, keys = pl.pallas_call(
        exchange,
        name="exchange",
        out_shape=(
            jax.ShapeDtypeStruct((16, WIN, IMG, UNITS * TILE), BF16),
            jax.ShapeDtypeStruct((8, 128), I32),
        ),
        in_specs=[any_, any_, vmem, pl.BlockSpec(memory_space=pltpu.SMEM), vmem],
        out_specs=(any_, vmem),
        scratch_shapes=[
            pltpu.VMEM((16, 2 * ROWS, K), BF16),
            pltpu.VMEM((8, 2, 2, 144, UNITS * TILE), BF16),
        ]
        + [pltpu.VMEM((64 * IMGS, IMG, TILE), BF16)] * UNITS
        + [
            pltpu.VMEM((UNITS, 16, WIN, IMG, TILE), BF16),
            pltpu.VMEM((256, 256), F32),
            pltpu.VMEM((HALF, 256), F32),
            pltpu.VMEM((8, 640), F32),
            pltpu.VMEM((8, 640), F32),
            pltpu.VMEM((32, 8, 128), I32),
            pltpu.VMEM((16, 8, 128), I32),
            pltpu.SMEM((16, 8, 128), I32),
            pltpu.SemaphoreType.DMA((SENDS,)),
            pltpu.SemaphoreType.DMA((SENDS,)),
            pltpu.SemaphoreType.DMA((2,)),
            pltpu.SemaphoreType.DMA((2, 3)),
            pltpu.SemaphoreType.DMA((2, 3)),
            pltpu.SemaphoreType.DMA((16,)),
            pltpu.SemaphoreType.DMA((16,)),
            pltpu.SemaphoreType.DMA((UNITS, 16)),
            pltpu.SemaphoreType.DMA((UNITS, 16)),
        ],
        compiler_params=pltpu.CompilerParams(
            collective_id=0, has_side_effects=True, vmem_limit_bytes=60 << 20
        ),
        cost_estimate=pl.CostEstimate(
            flops=2 * 2 * 448 * K * 640, bytes_accessed=8 << 20, transcendentals=0
        ),
    )(vit, merge_weight, merge_bias, image_sequence, tokens)
    count = residual.shape[1]
    return pl.pallas_call(
        finish,
        name="finish",
        grid=(2, 2),
        out_shape=jax.ShapeDtypeStruct(residual.shape, BF16),
        in_specs=[
            pl.BlockSpec((8, 128), lambda i, j: (0, 0)),
            pl.BlockSpec((16, WIN, IMG, UNITS * TILE), lambda i, j: (0, 0, 0, 0)),
            pl.BlockSpec((1, count // 2, 5120), lambda i, j: (i, j, 0)),
            pl.BlockSpec((2, 5120), lambda i, j: (0, 0)),
        ],
        out_specs=pl.BlockSpec((1, count // 2, 5120), lambda i, j: (i, j, 0)),
        compiler_params=pltpu.CompilerParams(vmem_limit_bytes=60 << 20),
    )(keys, arrived, residual, norm_gain)


def solution(mesh):
    return jax.shard_map(
        per_device,
        mesh=mesh,
        in_specs=(
            P(None, ("enc", "tp"), None),
            P(None, "enc", "tp"),
            P(None, "tp"),
            P(None, ("enc", "tp"), None),
            P(),
            P("enc"),
            P("enc"),
        ),
        out_specs=P(None, ("enc", "tp"), None),
        check_vma=False,
    )
```

```python
import functools

import jax
import jax.numpy as jnp
from jax import lax
from jax.experimental import pallas as pl
from jax.experimental.pallas import tpu as pltpu
from jax.sharding import PartitionSpec as P

MESH = pl.DeviceIdType.MESH
BF16, F32, I32 = jnp.bfloat16, jnp.float32, jnp.int32

IMG = 16
WIN = 17
ROWS = 56
IMGS = 14
HALF = IMGS * IMG
K = 4608
TILE = 128
UNITS = 5
SENDS = 300


def place(enc, tp):
    z_lo, rest = lax.div(enc, 8), lax.rem(enc, 8)
    return z_lo, lax.div(rest, 2), lax.rem(rest, 2), lax.div(tp, 4), lax.rem(tp, 4)


def device(z_lo, x, core, z_hi, y):
    return (z_lo * 8 + x * 2 + core, z_hi * 4 + y)


def running(values):
    count = values.shape[0]
    row = lax.broadcasted_iota(I32, values.shape, 0)
    total = values
    step = 1
    while step < count:
        total = total + jnp.where(row >= step, pltpu.roll(total, step, 0), 0)
        step *= 2
    return total - values


def exchange(
    vit, w, bias, images, tokens,
    arrived, keys,
    held, weight, g0, g1, g2, g3, g4, staged, acc, joined, own_bias, other_bias, table, lists, list_s,
    ssem, rsem, lsem, ws, wr, ls, lr, ds, dr,
):
    gathered = (g0, g1, g2, g3, g4)
    enc, tp = lax.axis_index("enc"), lax.axis_index("tp")
    z_lo, x, core, z_hi, y = place(enc, tp)
    z = z_hi * 4 + z_lo
    odd = lax.rem(x, 2)
    x_half = lax.div(x, 2)

    def at_xy(dx, dy):
        return device(z_lo, lax.rem(x + dx + 4, 4), core, z_hi, lax.rem(y + dy + 4, 4))

    def at_z(d):
        there = lax.rem(z + d + 8, 8)
        return device(lax.rem(there, 4), x, core, lax.div(there, 4), y)

    sibling = device(z_lo, x, 1 - core, z_hi, y)
    across = device(z_lo, x, core, 1 - z_hi, y)

    def at_lo(d):
        return device(lax.rem(z_lo + d, 4), x, core, z_hi, y)

    def scatter_to(b, i):
        side = 1 - z_hi if i == 2 else z_hi
        return device(z_lo, 2 * side + b, core, z_hi, y)

    far = x_half != z_hi

    barrier = pltpu.get_barrier_semaphore()
    peers = [at_xy(d // 4, d % 4) for d in range(1, 16)]
    peers += [at_z(1), at_z(-1), sibling, across] + [at_lo(d) for d in (1, 2, 3)]
    for peer in peers:
        pl.semaphore_signal(barrier, inc=1, device_id=peer, device_id_type=MESH)
    pl.semaphore_wait(barrier, len(peers))

    sends = {}

    def descriptor(key):
        number, like, _ = sends[key]
        return pltpu.make_async_remote_copy(
            src_ref=like(), dst_ref=like(), send_sem=ssem.at[number], recv_sem=rsem.at[number],
            device_id=sibling, device_id_type=MESH,
        )

    def put(key, src, like, to, dst=None, when=None):
        number = sends.setdefault(key, (len(sends), like, when))[0]
        pltpu.make_async_remote_copy(
            src_ref=src, dst_ref=like() if dst is None else dst, send_sem=ssem.at[number],
            recv_sem=rsem.at[number], device_id=to, device_id_type=MESH,
        ).start()

    def got(key, dst):
        number = sends[key][0]
        pltpu.make_async_remote_copy(
            src_ref=dst, dst_ref=dst, send_sem=ssem.at[number], recv_sem=rsem.at[number],
            device_id=sibling, device_id_type=MESH,
        ).wait_recv()

    part = K // 2

    def block(level, p, rx, ry, half=None):
        rows = pl.ds(0, 64) if level == 0 else pl.ds(64, 48)
        if half is None:
            return held.at[rx * 4 + ry, rows, pl.ds(p * part, part)]
        return held.at[rx * 4 + ry, rows, pl.ds(p * part + half * (part // 2), part // 2)]

    def near(p, first, second):
        return (second, first) if p == 0 else (first, second)

    def step_to(p, axis, d):
        return at_xy(*(near(p, d, 0) if axis == 0 else near(p, 0, d)))

    def send_block(level, p, axis, d, first, second, half=None, src=None):
        if axis == 0:
            there = ((first - d) % 4, second)
        else:
            there = (first, (second - d) % 4)
        src = block(level, p, *near(p, first, second), half) if src is None else src
        put(("v", level, p, there, half), src, lambda: block(level, p, *near(p, *there), half), step_to(p, axis, d))

    def have(level, p, first, second, half=None):
        got(("v", level, p, (first, second), half), block(level, p, *near(p, first, second), half))

    def vit_own(level, ways=((0, 0), (0, 1), (1, 0), (1, 1))):
        rows = pl.ds(0, 64) if level == 0 else pl.ds(64, 48)
        for axis, p in ways:
            if True:
                for d in (1, -1):
                    send_block(level, p, axis, d, 0, 0, src=vit.at[rows, pl.ds(p * part, part)])

    def vit_step(level, number):
        both = (0, 1)
        if number == 1:
            for p in both:
                for d in (1, -1):
                    off = (-d) % 4
                    have(level, p, off, 0)
                    send_block(level, p, 0, d, off, 0, half=0 if d == 1 else 1)
                    for d2 in (1, -1):
                        send_block(level, p, 1, d2, off, 0)
        if number == 2:
            for p in both:
                for d in (1, -1):
                    off = (-d) % 4
                    have(level, p, 0, off)
                    send_block(level, p, 1, d, 0, off, half=0 if d == 1 else 1)
        if number == 3:
            for p in both:
                for half in both:
                    have(level, p, 2, 0, half)
                for d2 in (1, -1):
                    send_block(level, p, 1, d2, 2, 0)
        if number in (4, 5):
            for first in ((3,) if number == 4 else (1,)):
                for p in both:
                    for d in (1, -1):
                        off = (-d) % 4
                        have(level, p, first, off)
                        send_block(level, p, 1, d, first, off, half=0 if d == 1 else 1)
        if number == 6:
            for p in both:
                for d in (1, -1):
                    off = (-d) % 4
                    have(level, p, 2, off)
                    send_block(level, p, 1, d, 2, off, half=0 if d == 1 else 1)
        if number in (7, 8):
            for first in ((0,) if number == 7 else (3, 1, 2)):
                for p in both:
                    for half in both:
                        have(level, p, first, 2, half)

    mine_w = weight.at[z_lo * 2 + x_half, odd, core]

    def scatter_parts(b):
        return (
            (w.at[0, :, pl.ds(384 * b, 256)], mine_w.at[:, pl.ds(0, 256)]),
            (w.at[b, :, pl.ds(256, 128)], mine_w.at[:, pl.ds(256, 128)]),
            (w.at[1, :, pl.ds(384 * b, 256)], mine_w.at[:, pl.ds(384, 256)]),
        )

    def scatter_copy(b, i):
        src, dst = scatter_parts(b)[i]
        return pltpu.make_async_remote_copy(
            src_ref=src, dst_ref=dst, send_sem=ws.at[b, i], recv_sem=wr.at[x, i],
            device_id=scatter_to(b, i), device_id_type=MESH,
        )

    def stays(b, i):
        return jnp.logical_and(odd == b, far if i == 2 else jnp.logical_not(far))

    def weight_scatter():
        for b in range(2):
            for i in range(3):
                @pl.when(stays(b, i))
                def _():
                    src, dst = scatter_parts(b)[i]
                    pltpu.make_async_copy(src, dst, wr.at[x, i]).start()

                @pl.when(jnp.logical_not(stays(b, i)))
                def _():
                    scatter_copy(b, i).start()

    def weight_scatter_wait():
        for b in range(2):
            for i in range(3):
                @pl.when(jnp.logical_not(stays(b, i)))
                def _():
                    scatter_copy(b, i).wait_send()

    wide = ((0, 384), (384, 256))

    def half_of(d):
        return lax.div(lax.rem(z + d + 8, 8), 4)

    begins = [
        {d: half_of(d) == (x_half if part_ == 0 else 1 - x_half) for d in range(-4, 5)} for part_ in range(2)
    ]

    def ring_send(kind, view, d, up, when=None):
        to = at_z(1) if up else at_z(-1)
        there = d - 1 if up else d + 1
        half = None if abs(there) < 4 else 0 if up else 1
        put((kind, there), view(d, half), lambda: view(d, half), to, when=when)

    def core_send(kind, view, d, when=None):
        put((kind, "core", d), view(d, None), lambda: view(d, None), sibling, when=when)

    def weight_view(part_, whose):
        cols = pl.ds(*wide[part_])

        def view(d, half):
            index = lax.rem(z + d + 8, 4) * 2
            if half is None:
                return weight.at[pl.ds(index, 2), :, whose, :, cols]
            return weight.at[index + half, :, whose, :, cols]
        return view

    def weight_step(part_, number):
        view = weight_view(part_, core)
        kind = ("w", part_)
        begin = begins[part_]
        if number == 0:
            @pl.when(begin[0])
            def _():
                for i in range(4):
                    for k, cols in (((0, (0, 256)), (1, (256, 128))), ((2, (384, 256)),))[part_]:
                        landing = weight.at[z_lo * 2 + i // 2, i % 2, core, :, pl.ds(*cols)]
                        pltpu.make_async_remote_copy(
                            src_ref=landing, dst_ref=landing, send_sem=ws.at[0, k], recv_sem=wr.at[i, k],
                            device_id=sibling, device_id_type=MESH,
                        ).wait_recv()
                for up in (True, False):
                    ring_send(kind, view, 0, up, begin[0])
                core_send(kind, view, 0, begin[0])
        elif number < 4:
            for d, up in ((-number, True), (number, False)):
                @pl.when(begin[d])
                def _():
                    got((kind, d), view(d, None))
                    ring_send(kind, view, d, up, begin[d])
                    core_send(kind, view, d, begin[d])
        elif number == 4:
            @pl.when(begin[4])
            def _():
                got((kind, -4), view(-4, 0))
                got((kind, 4), view(4, 1))
                core_send(kind, view, 4, begin[4])
        else:
            for d in (0, -1, 1, -2, 2, -3, 3, 4):
                @pl.when(begin[d])
                def _():
                    got((kind, "core", d), weight_view(part_, 1 - core)(d, None))

    def ring_step(kind, view, number):
        if number < 4:
            for d, up in ((-number, True), (number, False)):
                got((kind, d), view(d, None))
                ring_send(kind, view, d, up)
                core_send(kind, view, d)
        else:
            got((kind, -4), view(-4, 0))
            got((kind, 4), view(4, 1))
            core_send(kind, view, 4)

    def merged_view(g, group, d, half, whose):
        count = IMGS if group == 0 else 3 * IMGS
        start = (whose * 8 + lax.rem(z + d + 8, 8)) * (4 * IMGS) + group * IMGS
        if half is None:
            return g.at[pl.ds(start, count)]
        return g.at[pl.ds(start + half * (count // 2), count // 2)]

    def unit_step(unit, group, number):
        kind = ("g", unit, group)

        def view(d, half):
            return merged_view(gathered[unit], group, d, half, core)

        if number == 0:
            for up in (True, False):
                ring_send(kind, view, 0, up)
            core_send(kind, view, 0)
        elif number < 5:
            ring_step(kind, view, number)
        else:
            for d in (0, -1, 1, -2, 2, -3, 3, 4):
                got((kind, "core", d), merged_view(gathered[unit], group, d, None, 1 - core))

    def project(group, level, column, width, units, bias_row):
        def one(r, _):
            def chunk(k, _):
                rows = held[pl.ds(r * 4, 4), pl.ds(pl.multiple_of(level * 48, 16), 64),
                            pl.ds(pl.multiple_of(k * part, TILE), part)]
                cols = weight[pl.ds(k * 4, 4), :, :, :, column:column + width]
                product = jnp.dot(
                    rows.reshape(256, part), cols.reshape(part, width), preferred_element_type=F32
                )

                @pl.when(k == 0)
                def _():
                    acc[:, :width] = product

                @pl.when(k != 0)
                def _():
                    acc[:, :width] += product
                return 0

            lax.fori_loop(0, 2, chunk, 0)
            for ry in range(4):
                start = pl.multiple_of(lax.rem(y + ry, 4) * ROWS, 8)
                joined[pl.ds(start, ROWS), :width] = acc[
                    pl.ds(pl.multiple_of(ry * 64 + level * 8, 8), ROWS), :width
                ]
            start = ((core * 8 + z) * 4 + r) * IMGS
            for i, unit in enumerate(units):
                cols = slice(i * TILE, (i + 1) * TILE)
                gathered[unit][pl.ds(start, IMGS)] = (
                    joined[:, cols] + bias_row[:, cols]
                ).astype(BF16).reshape(IMGS, IMG, TILE)
            return 0

        lax.fori_loop(*((0, 1) if group == 0 else (1, 4)), one, 0)

    def bias_of(level, column, width):
        mine = jnp.where(jnp.logical_xor(far, column is None and level == 1), other_bias[...], own_bias[...])
        row = jnp.where(level == 0, mine[0:1], mine[1:2])
        if column is None:
            return jnp.where(odd == 0, row[:, 0:width], row[:, 384:384 + width])
        return row[:, column:column + width]

    def window_send(unit):
        g = gathered[unit]

        def one(d, _):
            dx, dy = lax.div(d, 4), lax.rem(d, 4)
            there = lax.rem(x + dx, 4) * 4 + lax.rem(y + dy, 4)
            for k in range(WIN):
                staged[unit, d, k] = g[list_s[there, 0, k]]
            dst = arrived.at[unit, x * 4 + y]

            @pl.when(d == 0)
            def _():
                pltpu.make_async_copy(staged.at[unit, d], dst, dr.at[unit, d]).start()

            @pl.when(d != 0)
            def _():
                pltpu.make_async_remote_copy(
                    src_ref=staged.at[unit, d], dst_ref=dst, send_sem=ds.at[unit, d], recv_sem=dr.at[unit, d],
                    device_id=at_xy(dx, dy), device_id_type=MESH,
                ).start()
            return 0

        lax.fori_loop(0, 16, one, 0)

    def window_wait(unit):
        dst0 = arrived.at[unit, x * 4 + y]
        pltpu.make_async_copy(staged.at[unit, 0], dst0, dr.at[unit, 0]).wait()

        def one(d, _):
            dx, dy = lax.div(d, 4), lax.rem(d, 4)
            here = lax.rem(x - dx + 4, 4) * 4 + lax.rem(y - dy + 4, 4)
            copy = pltpu.make_async_remote_copy(
                src_ref=staged.at[unit, d], dst_ref=arrived.at[unit, here],
                send_sem=ds.at[unit, d], recv_sem=dr.at[unit, d],
                device_id=at_xy(dx, dy), device_id_type=MESH,
            )
            copy.wait_send()
            copy.wait_recv()
            return 0

        lax.fori_loop(1, 16, one, 0)

    lane = lax.broadcasted_iota(I32, (32, 128), 1)
    sub = lax.broadcasted_iota(I32, (32, 128), 0)

    def own_table():
        of = jnp.full((32, 128), -1, I32)
        for i in range(2 * IMGS):
            of = jnp.where(sub == i, images[i], of)
        ours = jnp.where(of == lax.div(lane, 2), 1, 0)
        second = jnp.where(sub >= 14, 1, 0)
        where = ((core * 8 + second * 4 + z_lo) * 16 + sub - IMGS * second) * 4 + x
        pick = jnp.logical_and(ours == 1, running(ours) == lax.rem(lane, 2))
        row = jnp.sum(jnp.where(pick, where, 0), axis=0, keepdims=True)
        table[enc] = jnp.broadcast_to(row, (8, 128))

    def own_list():
        here = [tokens[pl.ds(tp * 2 + i, 1), :] for i in range(2)]
        slots = [lax.shift_right_arithmetic(row, 4) for row in here]
        total = jnp.zeros((1, 128), I32)
        picked = jnp.zeros((1, 128), I32)
        key = [jnp.zeros((1, 128), I32) for _ in range(2)]
        for rank in range(2):
            hit = [jnp.where(row == sub * 2 + rank, 1, 0) for row in slots]
            present = jnp.max(jnp.maximum(hit[0], hit[1]), axis=1, keepdims=True)
            present = jnp.broadcast_to(present, (32, 128))
            position = running(present) + total
            total = total + jnp.sum(present, axis=0, keepdims=True)
            places = jnp.where(lane == enc * 2 + rank, table[:, 0, :], 0)
            places = jnp.sum(places, axis=1, keepdims=True)
            chosen = jnp.logical_and(present == 1, position == lane)
            picked = picked + jnp.sum(jnp.where(chosen, places, 0), axis=0, keepdims=True)
            for i in range(2):
                key[i] = key[i] + jnp.sum(hit[i] * position, axis=0, keepdims=True)
        lists[x * 4 + y] = jnp.broadcast_to(picked, (8, 128))
        for i in range(2):
            keys[i:i + 1, :] = jnp.where(here[i] < 0, -1, key[i] * IMG + jnp.bitwise_and(here[i], IMG - 1))

    def list_copy(d, back):
        dx, dy = lax.div(d, 4), lax.rem(d, 4)
        sign = -1 if back else 1
        slot = lax.rem(x - dx + 4, 4) * 4 + lax.rem(y - dy + 4, 4) if back else x * 4 + y
        return pltpu.make_async_remote_copy(
            src_ref=lists.at[x * 4 + y], dst_ref=lists.at[slot], send_sem=ls.at[d], recv_sem=lr.at[d],
            device_id=at_xy(dx, dy), device_id_type=MESH,
        )

    def list_send():
        def one(d, _):
            list_copy(d, False).start()
            return 0
        lax.fori_loop(1, 16, one, 0)

    def list_wait():
        def one(d, _):
            copy = list_copy(d, True)
            copy.wait_send()
            copy.wait_recv()
            return 0
        lax.fori_loop(1, 16, one, 0)
        value = lists[...]
        r = jnp.bitwise_and(jnp.bitwise_and(value, 3) + (4 - x), 3)
        image = jnp.bitwise_and(lax.shift_right_logical(value, 2), 15)
        lists[...] = (lax.shift_right_logical(value, 6) * 4 + r) * IMGS + image
        copy = pltpu.make_async_copy(lists, list_s, lsem.at[1])
        copy.start()
        copy.wait()

    weight_scatter()
    vit_own(0)
    mine = pltpu.make_async_copy(vit, held.at[0], lsem.at[0])
    mine.start()
    own_table()
    own_bias[...] = jnp.zeros((8, 640), F32)
    own_bias[0:2, :] = bias[...].astype(F32)
    own = table.at[enc]
    put("one", own, lambda: own, sibling)
    put("bias", own_bias, lambda: other_bias, across)
    weight_step(0, 0)
    weight_step(1, 0)
    vit_step(0, 1)
    weight_step(0, 1)
    weight_step(1, 1)
    vit_step(0, 2)
    got("one", table.at[z_lo * 8 + x * 2 + 1 - core])
    pair = table.at[pl.ds(z_lo * 8 + x * 2, 2)]
    for d in (1, 2, 3):
        put(("pair", d), pair, lambda: pair, at_xy(d, 0))
    weight_step(0, 2)
    weight_step(1, 2)
    weight_step(0, 3)
    weight_step(1, 3)
    vit_step(0, 3)
    vit_step(0, 4)
    vit_step(0, 5)
    weight_step(0, 4)
    weight_step(1, 4)
    for d in (1, 2, 3):
        got(("pair", d), table.at[pl.ds(z_lo * 8 + lax.rem(x - d + 4, 4) * 2, 2)])
    eight = table.at[pl.ds(z_lo * 8, 8)]
    for d in (1, 2, 3):
        put(("eight", d), eight, lambda: eight, at_lo(d))
    vit_step(0, 7)
    weight_step(0, 5)
    weight_step(1, 5)
    mine.wait()
    got("bias", other_bias)
    a = (0, 0, 256, (0, 1), bias_of(0, None, 256))
    project(0, *a)
    unit_step(0, 0, 0)
    unit_step(1, 0, 0)
    unit_step(0, 0, 1)
    unit_step(1, 0, 1)
    vit_step(0, 6)
    vit_own(1)
    unit_step(0, 0, 2)
    unit_step(1, 0, 2)
    unit_step(0, 0, 3)
    unit_step(1, 0, 3)
    vit_step(0, 8)
    project(1, *a)
    unit_step(0, 1, 0)
    unit_step(1, 1, 0)
    unit_step(0, 0, 4)
    unit_step(1, 0, 4)
    for d in (1, 2, 3):
        got(("eight", d), table.at[pl.ds(lax.rem(z_lo - d + 4, 4) * 8, 8)])
    own_list()
    list_send()

    def window(unit):
        unit_step(unit, 0, 5)
        unit_step(unit, 1, 5)
        window_send(unit)

    def rest(even):
        b = (0 if even else 1, 256, 128, (2,), bias_of(0 if even else 1, 256, 128))
        c = (1, 384, 256, (3, 4), bias_of(1, None, 256))
        few = (3, 4) if even else (2, 3, 4)

        def small(number):
            for unit in few:
                unit_step(unit, 0, number)

        vit_step(1, 1)
        vit_step(1, 2)
        if even:
            project(0, *b)
            project(1, *b)
        unit_step(0, 1, 1)
        unit_step(1, 1, 1)
        if even:
            unit_step(2, 0, 0)
            unit_step(2, 1, 0)
        unit_step(0, 1, 2)
        vit_step(1, 3)
        unit_step(1, 1, 2)
        vit_step(1, 7)
        vit_step(1, 4)
        vit_step(1, 5)
        if not even:
            project(0, *b)
            unit_step(2, 0, 0)
        project(0, *c)
        if even:
            unit_step(2, 0, 1)
            unit_step(2, 1, 1)
            vit_step(1, 6)
            unit_step(0, 1, 3)
            unit_step(1, 1, 3)
            unit_step(0, 1, 4)
            list_wait()
            window(0)
            vit_step(1, 8)
            unit_step(2, 0, 2)
            unit_step(2, 1, 2)
            unit_step(1, 1, 4)
            window(1)
            small(0)
            project(1, *c)
            unit_step(2, 0, 3)
            unit_step(2, 1, 3)
            unit_step(3, 1, 0)
            small(1)
            unit_step(2, 0, 4)
            unit_step(2, 1, 4)
            window(2)
            small(2)
            unit_step(3, 1, 1)
            small(3)
            unit_step(3, 1, 2)
            unit_step(4, 1, 0)
            small(4)
        else:
            unit_step(3, 0, 0)
            unit_step(4, 0, 0)
            vit_step(1, 6)
            unit_step(0, 1, 3)
            unit_step(1, 1, 3)
            small(1)
            unit_step(0, 1, 4)
            list_wait()
            window(0)
            vit_step(1, 8)
            project(1, *b)
            unit_step(2, 1, 0)
            unit_step(1, 1, 4)
            small(2)
            window(1)
            project(1, *c)
            unit_step(2, 1, 1)
            small(3)
            unit_step(2, 1, 2)
            unit_step(3, 1, 0)
            small(4)
            unit_step(2, 1, 3)
            unit_step(3, 1, 1)
            unit_step(2, 1, 4)
            window(2)
            unit_step(3, 1, 2)
            unit_step(4, 1, 0)
        unit_step(3, 1, 3)
        unit_step(4, 1, 1)
        unit_step(3, 1, 4)
        window(3)
        unit_step(4, 1, 2)
        unit_step(4, 1, 3)
        unit_step(4, 1, 4)
        window(4)

    @pl.when(odd == 0)
    def _():
        rest(True)

    @pl.when(odd == 1)
    def _():
        rest(False)

    for unit in range(UNITS):
        window_wait(unit)
    for key, (_, _, when) in sends.items():
        if when is None:
            descriptor(key).wait_send()
        else:
            @pl.when(when)
            def _():
                descriptor(key).wait_send()
    weight_scatter_wait()


def finish(keys, arrived, residual, gain, out, buffer, sem):
    level = pl.program_id(0)
    tokens = residual.shape[1]

    def fetch(part):
        units = pl.ds(*((0, 3), (3, 2))[part])
        return pltpu.make_async_copy(arrived.at[units], buffer.at[units], sem.at[part])

    @pl.when(level == 0)
    def _():
        fetch(0).start()
        fetch(1).start()

    key = jnp.concatenate([keys[0:1, :], keys[1:2, :]], axis=1)
    hot = jnp.where(lax.broadcasted_iota(I32, (WIN * IMG, tokens), 0) == key, 1.0, 0.0)
    hot = hot.T.astype(BF16)

    def for_level(lvl):
        fetch(lvl).wait()
        square = jnp.zeros((tokens, TILE), F32)

        def add(start, source, units, square):
            width = TILE * len(units)
            rows = [buffer[unit, source].reshape(WIN * IMG, TILE) for unit in units]
            rows = jnp.concatenate(rows, axis=1) if len(units) > 1 else rows[0]
            deep = jnp.dot(hot, rows, preferred_element_type=F32)
            total = (residual[0, :, start:start + width].astype(F32) + deep).astype(BF16)
            out[0, :, start:start + width] = total
            total = total.astype(F32)
            for i in range(0, width, TILE):
                piece = total[:, i:i + TILE]
                square = square + piece * piece
            return square

        for source in range(16):
            sx, sy = source // 4, source % 4
            base = ((sx // 2) * 4 + sy) * 640
            other = ((1 - sx // 2) * 4 + sy) * 640
            if lvl == 0:
                square = add(base + 384 * (sx % 2), source, (0, 1), square)
            else:
                square = add(other + 384 * (sx % 2), source, (3, 4), square)
            if sx % 2 == lvl:
                square = add(base + 256, source, (2,), square)
        mean = jnp.sum(square, axis=1, keepdims=True) * (1.0 / 5120)
        scale = lax.rsqrt(mean + 1e-06)
        for start in range(0, 5120, 512):
            cols = slice(start, start + 512)
            values = out[0, :, cols].astype(F32)
            out[0, :, cols] = (values * scale * gain[lvl:lvl + 1, cols].astype(F32)).astype(BF16)

    @pl.when(level == 0)
    def _():
        for_level(0)

    @pl.when(level == 1)
    def _():
        for_level(1)


def per_device(
    vit_hidden, merge_weight, merge_bias, residual, norm_gain, image_sequence, token_source
):
    vit = vit_hidden.reshape(2 * ROWS, K)
    tokens = token_source.reshape(16, 128)
    any_, vmem = pl.BlockSpec(memory_space=pl.ANY), pl.BlockSpec(memory_space=pltpu.VMEM)
    arrived, keys = pl.pallas_call(
        exchange,
        name="exchange",
        out_shape=(
            jax.ShapeDtypeStruct((UNITS, 16, WIN, IMG, TILE), BF16),
            jax.ShapeDtypeStruct((8, 128), I32),
        ),
        in_specs=[any_, any_, vmem, pl.BlockSpec(memory_space=pltpu.SMEM), vmem],
        out_specs=(any_, vmem),
        scratch_shapes=[
            pltpu.VMEM((16, 2 * ROWS, K), BF16),
            pltpu.VMEM((8, 2, 2, 144, UNITS * TILE), BF16),
        ]
        + [pltpu.VMEM((64 * IMGS, IMG, TILE), BF16)] * UNITS
        + [
            pltpu.VMEM((UNITS, 16, WIN, IMG, TILE), BF16),
            pltpu.VMEM((256, 256), F32),
            pltpu.VMEM((HALF, 256), F32),
            pltpu.VMEM((8, 640), F32),
            pltpu.VMEM((8, 640), F32),
            pltpu.VMEM((32, 8, 128), I32),
            pltpu.VMEM((16, 8, 128), I32),
            pltpu.SMEM((16, 8, 128), I32),
            pltpu.SemaphoreType.DMA((SENDS,)),
            pltpu.SemaphoreType.DMA((SENDS,)),
            pltpu.SemaphoreType.DMA((2,)),
            pltpu.SemaphoreType.DMA((2, 3)),
            pltpu.SemaphoreType.DMA((4, 3)),
            pltpu.SemaphoreType.DMA((16,)),
            pltpu.SemaphoreType.DMA((16,)),
            pltpu.SemaphoreType.DMA((UNITS, 16)),
            pltpu.SemaphoreType.DMA((UNITS, 16)),
        ],
        compiler_params=pltpu.CompilerParams(
            collective_id=0, has_side_effects=True, vmem_limit_bytes=60 << 20
        ),
        cost_estimate=pl.CostEstimate(
            flops=2 * 2 * 448 * K * 640, bytes_accessed=8 << 20, transcendentals=0
        ),
    )(vit, merge_weight, merge_bias, image_sequence, tokens)
    count = residual.shape[1]
    return pl.pallas_call(
        finish,
        name="finish",
        grid=(2,),
        out_shape=jax.ShapeDtypeStruct(residual.shape, BF16),
        in_specs=[
            pl.BlockSpec((8, 128), lambda i: (0, 0)),
            any_,
            pl.BlockSpec((1, count, 5120), lambda i: (i, 0, 0)),
            pl.BlockSpec((2, 5120), lambda i: (0, 0)),
        ],
        out_specs=pl.BlockSpec((1, count, 5120), lambda i: (i, 0, 0)),
        scratch_shapes=[
            pltpu.VMEM((UNITS, 16, WIN, IMG, TILE), BF16),
            pltpu.SemaphoreType.DMA((2,)),
        ],
        compiler_params=pltpu.CompilerParams(vmem_limit_bytes=60 << 20),
    )(keys, arrived, residual, norm_gain)


def solution(mesh):
    return jax.shard_map(
        per_device,
        mesh=mesh,
        in_specs=(
            P(None, ("enc", "tp"), None),
            P(None, "enc", "tp"),
            P(None, "tp"),
            P(None, ("enc", "tp"), None),
            P(),
            P("enc"),
            P("enc"),
        ),
        out_specs=P(None, ("enc", "tp"), None),
        check_vma=False,
    )
```

```python
import functools

import jax
import jax.numpy as jnp
from jax import lax
from jax.experimental import pallas as pl
from jax.experimental.pallas import tpu as pltpu
from jax.sharding import PartitionSpec as P

MESH = pl.DeviceIdType.MESH
BF16, F32, I32 = jnp.bfloat16, jnp.float32, jnp.int32

IMG = 16
WIN = 17
ROWS = 56
IMGS = 14
HALF = IMGS * IMG
K = 4608
TILE = 128
UNITS = 5
SENDS = 300


def place(enc, tp):
    z_lo, rest = lax.div(enc, 8), lax.rem(enc, 8)
    return z_lo, lax.div(rest, 2), lax.rem(rest, 2), lax.div(tp, 4), lax.rem(tp, 4)


def device(z_lo, x, core, z_hi, y):
    return (z_lo * 8 + x * 2 + core, z_hi * 4 + y)


def running(values):
    count = values.shape[0]
    row = lax.broadcasted_iota(I32, values.shape, 0)
    total = values
    step = 1
    while step < count:
        total = total + jnp.where(row >= step, pltpu.roll(total, step, 0), 0)
        step *= 2
    return total - values


def exchange(
    vit, w, bias, images, tokens,
    arrived, keys,
    held, weight, g0, g1, g2, g3, g4, staged, acc, joined, own_bias, other_bias, table, lists, list_s,
    ssem, rsem, lsem, ws, wr, ls, lr, ds, dr,
):
    gathered = (g0, g1, g2, g3, g4)
    enc, tp = lax.axis_index("enc"), lax.axis_index("tp")
    z_lo, x, core, z_hi, y = place(enc, tp)
    z = z_hi * 4 + z_lo
    odd = lax.rem(x, 2)
    x_half = lax.div(x, 2)

    def at_xy(dx, dy):
        return device(z_lo, lax.rem(x + dx + 4, 4), core, z_hi, lax.rem(y + dy + 4, 4))

    def at_z(d):
        there = lax.rem(z + d + 8, 8)
        return device(lax.rem(there, 4), x, core, lax.div(there, 4), y)

    sibling = device(z_lo, x, 1 - core, z_hi, y)
    across = device(z_lo, x, core, 1 - z_hi, y)

    def at_lo(d):
        return device(lax.rem(z_lo + d, 4), x, core, z_hi, y)

    def scatter_to(b, i):
        side = 1 - z_hi if i == 2 else z_hi
        return device(z_lo, 2 * side + b, core, z_hi, y)

    far = x_half != z_hi

    barrier = pltpu.get_barrier_semaphore()
    peers = [at_xy(d // 4, d % 4) for d in range(1, 16)]
    peers += [at_z(1), at_z(-1), sibling, across] + [at_lo(d) for d in (1, 2, 3)]
    for peer in peers:
        pl.semaphore_signal(barrier, inc=1, device_id=peer, device_id_type=MESH)
    pl.semaphore_wait(barrier, len(peers))

    sends = {}

    def descriptor(key):
        number, like, _ = sends[key]
        return pltpu.make_async_remote_copy(
            src_ref=like(), dst_ref=like(), send_sem=ssem.at[number], recv_sem=rsem.at[number],
            device_id=sibling, device_id_type=MESH,
        )

    def put(key, src, like, to, dst=None, when=None):
        number = sends.setdefault(key, (len(sends), like, when))[0]
        pltpu.make_async_remote_copy(
            src_ref=src, dst_ref=like() if dst is None else dst, send_sem=ssem.at[number],
            recv_sem=rsem.at[number], device_id=to, device_id_type=MESH,
        ).start()

    def got(key, dst):
        number = sends[key][0]
        pltpu.make_async_remote_copy(
            src_ref=dst, dst_ref=dst, send_sem=ssem.at[number], recv_sem=rsem.at[number],
            device_id=sibling, device_id_type=MESH,
        ).wait_recv()

    part = K // 2

    def block(level, p, rx, ry, half=None):
        rows = pl.ds(0, 64) if level == 0 else pl.ds(64, 48)
        if half is None:
            return held.at[rx * 4 + ry, rows, pl.ds(p * part, part)]
        return held.at[rx * 4 + ry, rows, pl.ds(p * part + half * (part // 2), part // 2)]

    def near(p, first, second):
        return (second, first) if p == 0 else (first, second)

    def step_to(p, axis, d):
        return at_xy(*(near(p, d, 0) if axis == 0 else near(p, 0, d)))

    def send_block(level, p, axis, d, first, second, half=None, src=None):
        if axis == 0:
            there = ((first - d) % 4, second)
        else:
            there = (first, (second - d) % 4)
        src = block(level, p, *near(p, first, second), half) if src is None else src
        put(("v", level, p, there, half), src, lambda: block(level, p, *near(p, *there), half), step_to(p, axis, d))

    def have(level, p, first, second, half=None):
        got(("v", level, p, (first, second), half), block(level, p, *near(p, first, second), half))

    def vit_own(level, ways=((0, 0), (0, 1), (1, 0), (1, 1))):
        rows = pl.ds(0, 64) if level == 0 else pl.ds(64, 48)
        for axis, p in ways:
            if True:
                for d in (1, -1):
                    send_block(level, p, axis, d, 0, 0, src=vit.at[rows, pl.ds(p * part, part)])

    def vit_step(level, number):
        both = (0, 1)
        if number == 1:
            for p in both:
                for d in (1, -1):
                    off = (-d) % 4
                    have(level, p, off, 0)
                    send_block(level, p, 0, d, off, 0, half=0 if d == 1 else 1)
                    for d2 in (1, -1):
                        send_block(level, p, 1, d2, off, 0)
        if number == 2:
            for p in both:
                for d in (1, -1):
                    off = (-d) % 4
                    have(level, p, 0, off)
                    send_block(level, p, 1, d, 0, off, half=0 if d == 1 else 1)
        if number == 3:
            for p in both:
                for half in both:
                    have(level, p, 2, 0, half)
                for d2 in (1, -1):
                    send_block(level, p, 1, d2, 2, 0)
        if number in (4, 5):
            for first in ((3,) if number == 4 else (1,)):
                for p in both:
                    for d in (1, -1):
                        off = (-d) % 4
                        have(level, p, first, off)
                        send_block(level, p, 1, d, first, off, half=0 if d == 1 else 1)
        if number == 6:
            for p in both:
                for d in (1, -1):
                    off = (-d) % 4
                    have(level, p, 2, off)
                    send_block(level, p, 1, d, 2, off, half=0 if d == 1 else 1)
        if number in (7, 8):
            for first in ((0,) if number == 7 else (3, 1, 2)):
                for p in both:
                    for half in both:
                        have(level, p, first, 2, half)

    mine_w = weight.at[z_lo * 2 + x_half, odd, core]

    def scatter_parts(b):
        return (
            (w.at[0, :, pl.ds(384 * b, 256)], mine_w.at[:, pl.ds(0, 256)]),
            (w.at[b, :, pl.ds(256, 128)], mine_w.at[:, pl.ds(256, 128)]),
            (w.at[1, :, pl.ds(384 * b, 256)], mine_w.at[:, pl.ds(384, 256)]),
        )

    def scatter_copy(b, i):
        src, dst = scatter_parts(b)[i]
        return pltpu.make_async_remote_copy(
            src_ref=src, dst_ref=dst, send_sem=ws.at[b, i], recv_sem=wr.at[x, i],
            device_id=scatter_to(b, i), device_id_type=MESH,
        )

    def stays(b, i):
        return jnp.logical_and(odd == b, far if i == 2 else jnp.logical_not(far))

    def weight_scatter():
        for b in range(2):
            for i in range(3):
                @pl.when(stays(b, i))
                def _():
                    src, dst = scatter_parts(b)[i]
                    pltpu.make_async_copy(src, dst, wr.at[x, i]).start()

                @pl.when(jnp.logical_not(stays(b, i)))
                def _():
                    scatter_copy(b, i).start()

    def weight_scatter_wait():
        for b in range(2):
            for i in range(3):
                @pl.when(jnp.logical_not(stays(b, i)))
                def _():
                    scatter_copy(b, i).wait_send()

    wide = ((0, 384), (384, 256))

    def half_of(d):
        return lax.div(lax.rem(z + d + 8, 8), 4)

    begins = [
        {d: half_of(d) == (x_half if part_ == 0 else 1 - x_half) for d in range(-4, 5)} for part_ in range(2)
    ]

    def ring_send(kind, view, d, up, when=None):
        to = at_z(1) if up else at_z(-1)
        there = d - 1 if up else d + 1
        half = None if abs(there) < 4 else 0 if up else 1
        put((kind, there), view(d, half), lambda: view(d, half), to, when=when)

    def core_send(kind, view, d, when=None):
        put((kind, "core", d), view(d, None), lambda: view(d, None), sibling, when=when)

    def weight_view(part_, whose):
        cols = pl.ds(*wide[part_])

        def view(d, half):
            index = lax.rem(z + d + 8, 4) * 2
            if half is None:
                return weight.at[pl.ds(index, 2), :, whose, :, cols]
            return weight.at[index + half, :, whose, :, cols]
        return view

    def weight_step(part_, number):
        view = weight_view(part_, core)
        kind = ("w", part_)
        begin = begins[part_]
        if number == 0:
            @pl.when(begin[0])
            def _():
                for i in range(4):
                    for k, cols in (((0, (0, 256)), (1, (256, 128))), ((2, (384, 256)),))[part_]:
                        landing = weight.at[z_lo * 2 + i // 2, i % 2, core, :, pl.ds(*cols)]
                        pltpu.make_async_remote_copy(
                            src_ref=landing, dst_ref=landing, send_sem=ws.at[0, k], recv_sem=wr.at[i, k],
                            device_id=sibling, device_id_type=MESH,
                        ).wait_recv()
                for up in (True, False):
                    ring_send(kind, view, 0, up, begin[0])
                core_send(kind, view, 0, begin[0])
        elif number < 4:
            for d, up in ((-number, True), (number, False)):
                @pl.when(begin[d])
                def _():
                    got((kind, d), view(d, None))
                    ring_send(kind, view, d, up, begin[d])
                    core_send(kind, view, d, begin[d])
        elif number == 4:
            @pl.when(begin[4])
            def _():
                got((kind, -4), view(-4, 0))
                got((kind, 4), view(4, 1))
                core_send(kind, view, 4, begin[4])
        else:
            for d in (0, -1, 1, -2, 2, -3, 3, 4):
                @pl.when(begin[d])
                def _():
                    got((kind, "core", d), weight_view(part_, 1 - core)(d, None))

    def ring_step(kind, view, number):
        if number < 4:
            for d, up in ((-number, True), (number, False)):
                got((kind, d), view(d, None))
                ring_send(kind, view, d, up)
                core_send(kind, view, d)
        else:
            got((kind, -4), view(-4, 0))
            got((kind, 4), view(4, 1))
            core_send(kind, view, 4)

    def merged_view(g, group, d, half, whose):
        count = IMGS if group == 0 else 3 * IMGS
        start = (whose * 8 + lax.rem(z + d + 8, 8)) * (4 * IMGS) + group * IMGS
        if half is None:
            return g.at[pl.ds(start, count)]
        return g.at[pl.ds(start + half * (count // 2), count // 2)]

    def unit_step(unit, group, number):
        kind = ("g", unit, group)

        def view(d, half):
            return merged_view(gathered[unit], group, d, half, core)

        if number == 0:
            for up in (True, False):
                ring_send(kind, view, 0, up)
            core_send(kind, view, 0)
        elif number < 5:
            ring_step(kind, view, number)
        else:
            for d in (0, -1, 1, -2, 2, -3, 3, 4):
                got((kind, "core", d), merged_view(gathered[unit], group, d, None, 1 - core))

    def project(group, level, column, width, units, bias_row):
        def one(r, _):
            def chunk(k, _):
                rows = held[pl.ds(r * 4, 4), pl.ds(pl.multiple_of(level * 48, 16), 64),
                            pl.ds(pl.multiple_of(k * part, TILE), part)]
                cols = weight[pl.ds(k * 4, 4), :, :, :, column:column + width]
                product = jnp.dot(
                    rows.reshape(256, part), cols.reshape(part, width), preferred_element_type=F32
                )

                @pl.when(k == 0)
                def _():
                    acc[:, :width] = product

                @pl.when(k != 0)
                def _():
                    acc[:, :width] += product
                return 0

            lax.fori_loop(0, 2, chunk, 0)
            for ry in range(4):
                start = pl.multiple_of(lax.rem(y + ry, 4) * ROWS, 8)
                joined[pl.ds(start, ROWS), :width] = acc[
                    pl.ds(pl.multiple_of(ry * 64 + level * 8, 8), ROWS), :width
                ]
            start = ((core * 8 + z) * 4 + r) * IMGS
            for i, unit in enumerate(units):
                cols = slice(i * TILE, (i + 1) * TILE)
                gathered[unit][pl.ds(start, IMGS)] = (
                    joined[:, cols] + bias_row[:, cols]
                ).astype(BF16).reshape(IMGS, IMG, TILE)
            return 0

        lax.fori_loop(*((0, 1) if group == 0 else (1, 4)), one, 0)

    def bias_of(level, column, width):
        mine = jnp.where(jnp.logical_xor(far, column is None and level == 1), other_bias[...], own_bias[...])
        row = jnp.where(level == 0, mine[0:1], mine[1:2])
        if column is None:
            return jnp.where(odd == 0, row[:, 0:width], row[:, 384:384 + width])
        return row[:, column:column + width]

    def window_send(unit):
        g = gathered[unit]

        def one(i, _):
            d = lax.rem(i * 7 + 10, 16)
            dx, dy = lax.div(d, 4), lax.rem(d, 4)
            there = lax.rem(x + dx, 4) * 4 + lax.rem(y + dy, 4)
            for k in range(WIN):
                staged[unit, d, k] = g[list_s[there, 0, k]]
            dst = arrived.at[unit, x * 4 + y]

            @pl.when(d == 0)
            def _():
                pltpu.make_async_copy(staged.at[unit, d], dst, dr.at[unit, d]).start()

            @pl.when(d != 0)
            def _():
                pltpu.make_async_remote_copy(
                    src_ref=staged.at[unit, d], dst_ref=dst, send_sem=ds.at[unit, d], recv_sem=dr.at[unit, d],
                    device_id=at_xy(dx, dy), device_id_type=MESH,
                ).start()
            return 0

        lax.fori_loop(0, 16, one, 0)

    def window_wait(unit):
        dst0 = arrived.at[unit, x * 4 + y]
        pltpu.make_async_copy(staged.at[unit, 0], dst0, dr.at[unit, 0]).wait()

        def one(d, _):
            dx, dy = lax.div(d, 4), lax.rem(d, 4)
            here = lax.rem(x - dx + 4, 4) * 4 + lax.rem(y - dy + 4, 4)
            copy = pltpu.make_async_remote_copy(
                src_ref=staged.at[unit, d], dst_ref=arrived.at[unit, here],
                send_sem=ds.at[unit, d], recv_sem=dr.at[unit, d],
                device_id=at_xy(dx, dy), device_id_type=MESH,
            )
            copy.wait_send()
            copy.wait_recv()
            return 0

        lax.fori_loop(1, 16, one, 0)

    lane = lax.broadcasted_iota(I32, (32, 128), 1)
    sub = lax.broadcasted_iota(I32, (32, 128), 0)

    def own_table():
        of = jnp.full((32, 128), -1, I32)
        for i in range(2 * IMGS):
            of = jnp.where(sub == i, images[i], of)
        ours = jnp.where(of == lax.div(lane, 2), 1, 0)
        second = jnp.where(sub >= 14, 1, 0)
        where = ((core * 8 + second * 4 + z_lo) * 16 + sub - IMGS * second) * 4 + x
        pick = jnp.logical_and(ours == 1, running(ours) == lax.rem(lane, 2))
        row = jnp.sum(jnp.where(pick, where, 0), axis=0, keepdims=True)
        table[enc] = jnp.broadcast_to(row, (8, 128))

    def own_list():
        here = [tokens[pl.ds(tp * 2 + i, 1), :] for i in range(2)]
        slots = [lax.shift_right_arithmetic(row, 4) for row in here]
        total = jnp.zeros((1, 128), I32)
        picked = jnp.zeros((1, 128), I32)
        key = [jnp.zeros((1, 128), I32) for _ in range(2)]
        for rank in range(2):
            hit = [jnp.where(row == sub * 2 + rank, 1, 0) for row in slots]
            present = jnp.max(jnp.maximum(hit[0], hit[1]), axis=1, keepdims=True)
            present = jnp.broadcast_to(present, (32, 128))
            position = running(present) + total
            total = total + jnp.sum(present, axis=0, keepdims=True)
            places = jnp.where(lane == enc * 2 + rank, table[:, 0, :], 0)
            places = jnp.sum(places, axis=1, keepdims=True)
            chosen = jnp.logical_and(present == 1, position == lane)
            picked = picked + jnp.sum(jnp.where(chosen, places, 0), axis=0, keepdims=True)
            for i in range(2):
                key[i] = key[i] + jnp.sum(hit[i] * position, axis=0, keepdims=True)
        lists[x * 4 + y] = jnp.broadcast_to(picked, (8, 128))
        for i in range(2):
            keys[i:i + 1, :] = jnp.where(here[i] < 0, -1, key[i] * IMG + jnp.bitwise_and(here[i], IMG - 1))

    def list_copy(d, back):
        dx, dy = lax.div(d, 4), lax.rem(d, 4)
        sign = -1 if back else 1
        slot = lax.rem(x - dx + 4, 4) * 4 + lax.rem(y - dy + 4, 4) if back else x * 4 + y
        return pltpu.make_async_remote_copy(
            src_ref=lists.at[x * 4 + y], dst_ref=lists.at[slot], send_sem=ls.at[d], recv_sem=lr.at[d],
            device_id=at_xy(dx, dy), device_id_type=MESH,
        )

    def list_send():
        def one(d, _):
            list_copy(d, False).start()
            return 0
        lax.fori_loop(1, 16, one, 0)

    def list_wait():
        def one(d, _):
            copy = list_copy(d, True)
            copy.wait_send()
            copy.wait_recv()
            return 0
        lax.fori_loop(1, 16, one, 0)
        value = lists[...]
        r = jnp.bitwise_and(jnp.bitwise_and(value, 3) + (4 - x), 3)
        image = jnp.bitwise_and(lax.shift_right_logical(value, 2), 15)
        lists[...] = (lax.shift_right_logical(value, 6) * 4 + r) * IMGS + image
        copy = pltpu.make_async_copy(lists, list_s, lsem.at[1])
        copy.start()
        copy.wait()

    weight_scatter()
    vit_own(0)
    mine = pltpu.make_async_copy(vit, held.at[0], lsem.at[0])
    mine.start()
    own_table()
    own_bias[...] = jnp.zeros((8, 640), F32)
    own_bias[0:2, :] = bias[...].astype(F32)
    own = table.at[enc]
    put("one", own, lambda: own, sibling)
    put("bias", own_bias, lambda: other_bias, across)
    weight_step(0, 0)
    weight_step(1, 0)
    vit_step(0, 1)
    weight_step(0, 1)
    weight_step(1, 1)
    vit_step(0, 2)
    got("one", table.at[z_lo * 8 + x * 2 + 1 - core])
    pair = table.at[pl.ds(z_lo * 8 + x * 2, 2)]
    for d in (1, 2, 3):
        put(("pair", d), pair, lambda: pair, at_xy(d, 0))
    weight_step(0, 2)
    weight_step(1, 2)
    weight_step(0, 3)
    weight_step(1, 3)
    vit_step(0, 3)
    vit_step(0, 4)
    vit_step(0, 5)
    weight_step(0, 4)
    weight_step(1, 4)
    for d in (1, 2, 3):
        got(("pair", d), table.at[pl.ds(z_lo * 8 + lax.rem(x - d + 4, 4) * 2, 2)])
    eight = table.at[pl.ds(z_lo * 8, 8)]
    for d in (1, 2, 3):
        put(("eight", d), eight, lambda: eight, at_lo(d))
    vit_step(0, 7)
    weight_step(0, 5)
    weight_step(1, 5)
    mine.wait()
    got("bias", other_bias)
    a = (0, 0, 256, (0, 1), bias_of(0, None, 256))
    project(0, *a)
    unit_step(0, 0, 0)
    unit_step(1, 0, 0)
    unit_step(0, 0, 1)
    unit_step(1, 0, 1)
    vit_step(0, 6)
    vit_own(1)
    unit_step(0, 0, 2)
    unit_step(1, 0, 2)
    unit_step(0, 0, 3)
    unit_step(1, 0, 3)
    vit_step(0, 8)
    project(1, *a)
    unit_step(0, 1, 0)
    unit_step(1, 1, 0)
    unit_step(0, 0, 4)
    unit_step(1, 0, 4)
    for d in (1, 2, 3):
        got(("eight", d), table.at[pl.ds(lax.rem(z_lo - d + 4, 4) * 8, 8)])
    own_list()
    list_send()

    def window(unit):
        unit_step(unit, 0, 5)
        unit_step(unit, 1, 5)
        window_send(unit)

    def rest(even):
        b = (0 if even else 1, 256, 128, (2,), bias_of(0 if even else 1, 256, 128))
        c = (1, 384, 256, (3, 4), bias_of(1, None, 256))
        few = (3, 4) if even else (2, 3, 4)

        def small(number):
            for unit in few:
                unit_step(unit, 0, number)

        vit_step(1, 1)
        vit_step(1, 2)
        if even:
            project(0, *b)
            project(1, *b)
        unit_step(0, 1, 1)
        unit_step(1, 1, 1)
        if even:
            unit_step(2, 0, 0)
            unit_step(2, 1, 0)
        unit_step(0, 1, 2)
        vit_step(1, 3)
        unit_step(1, 1, 2)
        vit_step(1, 7)
        vit_step(1, 4)
        vit_step(1, 5)
        if not even:
            project(0, *b)
            unit_step(2, 0, 0)
        project(0, *c)
        if even:
            unit_step(2, 0, 1)
            unit_step(2, 1, 1)
            vit_step(1, 6)
            unit_step(0, 1, 3)
            unit_step(1, 1, 3)
            unit_step(0, 1, 4)
            list_wait()
            window(0)
            vit_step(1, 8)
            unit_step(2, 0, 2)
            unit_step(2, 1, 2)
            unit_step(1, 1, 4)
            window(1)
            small(0)
            project(1, *c)
            unit_step(2, 0, 3)
            unit_step(2, 1, 3)
            unit_step(3, 1, 0)
            small(1)
            unit_step(2, 0, 4)
            unit_step(2, 1, 4)
            window(2)
            small(2)
            unit_step(3, 1, 1)
            small(3)
            unit_step(3, 1, 2)
            unit_step(4, 1, 0)
            small(4)
        else:
            unit_step(3, 0, 0)
            unit_step(4, 0, 0)
            vit_step(1, 6)
            unit_step(0, 1, 3)
            unit_step(1, 1, 3)
            small(1)
            unit_step(0, 1, 4)
            list_wait()
            window(0)
            vit_step(1, 8)
            project(1, *b)
            unit_step(2, 1, 0)
            unit_step(1, 1, 4)
            small(2)
            window(1)
            project(1, *c)
            unit_step(2, 1, 1)
            small(3)
            unit_step(2, 1, 2)
            unit_step(3, 1, 0)
            small(4)
            unit_step(2, 1, 3)
            unit_step(3, 1, 1)
            unit_step(2, 1, 4)
            window(2)
            unit_step(3, 1, 2)
            unit_step(4, 1, 0)
        unit_step(3, 1, 3)
        unit_step(4, 1, 1)
        unit_step(3, 1, 4)
        window(3)
        unit_step(4, 1, 2)
        unit_step(4, 1, 3)
        unit_step(4, 1, 4)
        window(4)

    @pl.when(odd == 0)
    def _():
        rest(True)

    @pl.when(odd == 1)
    def _():
        rest(False)

    for unit in range(UNITS):
        window_wait(unit)
    for key, (_, _, when) in sends.items():
        if when is None:
            descriptor(key).wait_send()
        else:
            @pl.when(when)
            def _():
                descriptor(key).wait_send()
    weight_scatter_wait()


def finish(keys, arrived, residual, gain, out, buffer, stream, result, sem, out_sem):
    tokens = residual.shape[1]
    half = tokens // 2
    fetches = []
    for lvl in range(2):
        units = pl.ds(*((0, 3), (3, 2))[lvl])
        fetches.append((
            pltpu.make_async_copy(residual.at[lvl], stream.at[lvl], sem.at[lvl, 0]),
            pltpu.make_async_copy(arrived.at[units], buffer.at[units], sem.at[lvl, 1]),
        ))
    for pair in fetches:
        for copy in pair:
            copy.start()

    key = jnp.concatenate([keys[0:1, :], keys[1:2, :]], axis=1)
    hot = jnp.where(lax.broadcasted_iota(I32, (WIN * IMG, tokens), 0) == key, 1.0, 0.0)
    hot = hot.T.astype(BF16)
    stores = []
    for lvl in range(2):
        for copy in fetches[lvl]:
            copy.wait()
        square = jnp.zeros((tokens, TILE), F32)

        def add(start, source, units, square):
            width = TILE * len(units)
            rows = [buffer[unit, source].reshape(WIN * IMG, TILE) for unit in units]
            rows = jnp.concatenate(rows, axis=1) if len(units) > 1 else rows[0]
            deep = jnp.dot(hot, rows, preferred_element_type=F32)
            total = (stream[lvl, :, start:start + width].astype(F32) + deep).astype(BF16)
            result[lvl, :, start:start + width] = total
            total = total.astype(F32)
            for i in range(0, width, TILE):
                piece = total[:, i:i + TILE]
                square = square + piece * piece
            return square

        for source in range(16):
            sx, sy = source // 4, source % 4
            base = ((sx // 2) * 4 + sy) * 640
            other = ((1 - sx // 2) * 4 + sy) * 640
            if lvl == 0:
                square = add(base + 384 * (sx % 2), source, (0, 1), square)
            else:
                square = add(other + 384 * (sx % 2), source, (3, 4), square)
            if sx % 2 == lvl:
                square = add(base + 256, source, (2,), square)
        mean = jnp.sum(square, axis=1, keepdims=True) * (1.0 / 5120)
        scale = lax.rsqrt(mean + 1e-06)
        for part in range(2):
            rows = slice(part * half, (part + 1) * half)
            for start in range(0, 5120, 512):
                cols = slice(start, start + 512)
                values = result[lvl, rows, cols].astype(F32)
                result[lvl, rows, cols] = (
                    values * scale[rows] * gain[lvl:lvl + 1, cols].astype(F32)
                ).astype(BF16)
            place_ = pl.ds(part * half, half)
            copy = pltpu.make_async_copy(result.at[lvl, place_], out.at[lvl, place_], out_sem.at[lvl, part])
            copy.start()
            stores.append(copy)
    for copy in stores:
        copy.wait()


def per_device(
    vit_hidden, merge_weight, merge_bias, residual, norm_gain, image_sequence, token_source
):
    vit = vit_hidden.reshape(2 * ROWS, K)
    tokens = token_source.reshape(16, 128)
    any_, vmem = pl.BlockSpec(memory_space=pl.ANY), pl.BlockSpec(memory_space=pltpu.VMEM)
    arrived, keys = pl.pallas_call(
        exchange,
        name="exchange",
        out_shape=(
            jax.ShapeDtypeStruct((UNITS, 16, WIN, IMG, TILE), BF16),
            jax.ShapeDtypeStruct((8, 128), I32),
        ),
        in_specs=[any_, any_, vmem, pl.BlockSpec(memory_space=pltpu.SMEM), vmem],
        out_specs=(any_, vmem),
        scratch_shapes=[
            pltpu.VMEM((16, 2 * ROWS, K), BF16),
            pltpu.VMEM((8, 2, 2, 144, UNITS * TILE), BF16),
        ]
        + [pltpu.VMEM((64 * IMGS, IMG, TILE), BF16)] * UNITS
        + [
            pltpu.VMEM((UNITS, 16, WIN, IMG, TILE), BF16),
            pltpu.VMEM((256, 256), F32),
            pltpu.VMEM((HALF, 256), F32),
            pltpu.VMEM((8, 640), F32),
            pltpu.VMEM((8, 640), F32),
            pltpu.VMEM((32, 8, 128), I32),
            pltpu.VMEM((16, 8, 128), I32),
            pltpu.SMEM((16, 8, 128), I32),
            pltpu.SemaphoreType.DMA((SENDS,)),
            pltpu.SemaphoreType.DMA((SENDS,)),
            pltpu.SemaphoreType.DMA((2,)),
            pltpu.SemaphoreType.DMA((2, 3)),
            pltpu.SemaphoreType.DMA((4, 3)),
            pltpu.SemaphoreType.DMA((16,)),
            pltpu.SemaphoreType.DMA((16,)),
            pltpu.SemaphoreType.DMA((UNITS, 16)),
            pltpu.SemaphoreType.DMA((UNITS, 16)),
        ],
        compiler_params=pltpu.CompilerParams(
            collective_id=0, has_side_effects=True, vmem_limit_bytes=60 << 20
        ),
        cost_estimate=pl.CostEstimate(
            flops=2 * 2 * 448 * K * 640, bytes_accessed=8 << 20, transcendentals=0
        ),
    )(vit, merge_weight, merge_bias, image_sequence, tokens)
    count = residual.shape[1]
    return pl.pallas_call(
        finish,
        name="finish",
        out_shape=jax.ShapeDtypeStruct(residual.shape, BF16),
        in_specs=[vmem, any_, any_, vmem],
        out_specs=any_,
        scratch_shapes=[
            pltpu.VMEM((UNITS, 16, WIN, IMG, TILE), BF16),
            pltpu.VMEM((2, count, 5120), BF16),
            pltpu.VMEM((2, count, 5120), BF16),
            pltpu.SemaphoreType.DMA((2, 2)),
            pltpu.SemaphoreType.DMA((2, 2)),
        ],
        compiler_params=pltpu.CompilerParams(vmem_limit_bytes=60 << 20),
    )(keys, arrived, residual, norm_gain)


def solution(mesh):
    return jax.shard_map(
        per_device,
        mesh=mesh,
        in_specs=(
            P(None, ("enc", "tp"), None),
            P(None, "enc", "tp"),
            P(None, "tp"),
            P(None, ("enc", "tp"), None),
            P(),
            P("enc"),
            P("enc"),
        ),
        out_specs=P(None, ("enc", "tp"), None),
        check_vma=False,
    )
```
